32 devices in a mesh: lang: 16 (over z, y, x), fsdp: 2 (over core).
Axes of the slice: x: 2, y: 2, z: 4, core: 2. Of those that a mesh axis runs over, the one named last changes fastest.
Arguments:
- tokens: bfloat16 [8192, 1920], P(('lang', 'fsdp')), may hold values from -6 to 6
- lengths: int32 [512], P(('lang', 'fsdp')), may hold values from 1 to 31, as said below
- target: int32 [512], P(('lang', 'fsdp')), may hold values from 0 to 201, as said below
- lang_group: int32 [202], replicated, may hold values from 0 to 15, as said below
- blocks: int32 [16, 2], P('lang', 'fsdp'), may hold values from 0 to 4, as said below
- enc_gain: float32 [1920], replicated, may hold values from 0.5 to 1.5
- w_query: bfloat16 [1920, 1024], P('fsdp'), may hold values from -1 to 1
- w_key: bfloat16 [1920, 1024], P('fsdp'), may hold values from -1 to 1
- w_value: bfloat16 [1920, 1024], P('fsdp'), may hold values from -0.125 to 0.125
- w_output: bfloat16 [1024, 1920], P('fsdp'), may hold values from -0.1875 to 0.1875
- moe_gain: float32 [1920], replicated, may hold values from 0.5 to 1.5
- expert_in: bfloat16 [16, 1920, 4096], P('lang', None, 'fsdp'), may hold values from -0.125 to 0.125
- expert_out: bfloat16 [16, 4096, 1920], P('lang', 'fsdp'), may hold values from -0.09375 to 0.09375
Outputs:
- mixed: bfloat16 [8192, 1920], P(('lang', 'fsdp'))
The draws below stay inside these ranges and needn't reach their ends.
Inputs may be any that keep to these rules, and one draw needn't show every extreme that they name: The lengths of one device sum to 256; its tokens come in 8 consecutive runs of 32 tokens, each run holding whole sentences. All sentences of one run of 32 tokens have target languages of one group, and the runs of one device have different groups. At most 512 tokens reach one group from the devices of one fsdp index, and for every fsdp index some group receives exactly 512. `lang_group`: every group has at least one language. blocks[g, f] is the number of tokens that reach group g from the devices of fsdp index f, divided by 128 and rounded up.
All inputs are finite; a program needn't handle non-finite values.
Results may differ from the reference program's by a relative error of at most 0.0066.
Values may be sent and summed in bfloat16 or wider, within the bound.
No kernel may reach another device: no remote copies, remote signals or barrier semaphores. Data moves between devices by JAX's collectives and lax.ppermute only.
A program may use at most 128 MiB of HBM per device.

```python
import jax
import jax.numpy as jnp
from jax import lax

D = 1920
HEADS = 8
HDIM = 128
FF = 4096
LANGS = 202
BLOCK = 128
TOK_DEV = 256
TARGET_GROUPS = 8
GROUP_TOKEN_LIMIT = 32
HOT = 16
GCAP = 512
EXPERTS = 16
TOKENS = 8192
N_LANG = 16
N_FSDP = 2


def route_plan(key):
    perm_lang = jax.random.permutation(jax.random.fold_in(key, 101), LANGS)
    group_of = (jnp.argsort(perm_lang) % N_LANG).astype(jnp.int32)

    def per_shard(shard_key):
        sort_keys = jax.random.split(shard_key, 5)
        perm_group = jax.random.permutation(sort_keys[0], N_LANG)
        perm_send = jax.random.permutation(sort_keys[1], N_LANG)
        ranked_entries = jnp.argsort(perm_send)
        column_entry = jnp.arange(TARGET_GROUPS)
        largest_groups = (ranked_entries[:, None] < HOT).astype(jnp.int32)
        sliding_span = 1 + (ranked_entries[:, None] * TARGET_GROUPS + column_entry[None, :] - largest_groups) % (N_LANG - 1)
        index = jnp.where((largest_groups == 1) & (column_entry[None, :] == 0), 0, sliding_span)
        groups = perm_group[index]
        destination_keys = jax.random.split(sort_keys[2], N_LANG)
        sorting_orders = jax.vmap(lambda single_item: jax.random.permutation(single_item, TARGET_GROUPS))(destination_keys)
        groups = jnp.take_along_axis(groups, sorting_orders, axis=1)
        leading_length = jax.random.randint(sort_keys[3], (N_LANG, TARGET_GROUPS), 1, GROUP_TOKEN_LIMIT)
        lens = jnp.stack([leading_length, GROUP_TOKEN_LIMIT - leading_length], axis=-1)
        counts = jnp.sum((groups[:, :, None] == jnp.arange(N_LANG)[None, None, :]).astype(jnp.int32), axis=(0, 1))
        pair_groups = jnp.stack([groups, groups], axis=-1)
        choices_left = (LANGS - 1 - pair_groups) // N_LANG + 1
        picks = jax.random.randint(sort_keys[4], pair_groups.shape, 0, choices_left)
        targets = perm_lang[pair_groups + N_LANG * picks]
        block_counts = (counts * GROUP_TOKEN_LIMIT + BLOCK - 1) // BLOCK
        return (lens, targets, block_counts)
    shard_keys = jax.random.split(jax.random.fold_in(key, 102), N_FSDP)
    lens, targets, block_counts = jax.vmap(per_shard)(shard_keys)
    lengths = jnp.transpose(lens, (1, 0, 2, 3)).reshape(-1).astype(jnp.int32)
    target = jnp.transpose(targets, (1, 0, 2, 3)).reshape(-1).astype(jnp.int32)
    return (lengths, target, group_of, jnp.transpose(block_counts).astype(jnp.int32))


def draw_lengths(key, part):
    return route_plan(key)[0]


def draw_target(key, part):
    return route_plan(key)[1]


def draw_lang_group(key, part):
    return route_plan(key)[2]


def draw_blocks(key, part):
    return route_plan(key)[3]


def attention_pair(key):
    shape = (D, HEADS * HDIM)
    base = jax.random.normal(jax.random.fold_in(key, 31), shape, jnp.float32)
    other = jax.random.normal(jax.random.fold_in(key, 33), shape, jnp.float32)
    factor = 1.0 / jnp.sqrt(jnp.float32(D))
    first = jnp.clip(base * factor, -1.0, 1.0)
    second = jnp.clip(other * factor, -1.0, 1.0)
    return (first, second)


def draw_w_query(key, part):
    return attention_pair(key)[0].astype(jnp.bfloat16)


def draw_w_key(key, part):
    return attention_pair(key)[1].astype(jnp.bfloat16)


def block_scale(rng, extent, cuts, smallest, largest):
    level, own = 1.0, jax.random.fold_in(rng, 6)
    for axis_at, shards_of in cuts:
        steps = jnp.exp(jax.random.uniform(jax.random.fold_in(own, axis_at), (shards_of,), jnp.float32, smallest / len(cuts), largest / len(cuts)))
        level = level * jnp.repeat(steps, extent[axis_at] // shards_of).reshape([-1 if axis == axis_at else 1 for axis in range(len(extent))])
    return level


def scatter_about(stream_key, extent, scale, limit, cuts=(), held_as=jnp.bfloat16):
    values = scale * jax.random.normal(stream_key, extent, jnp.float32)
    if cuts:
        values = values * block_scale(stream_key, extent, cuts, -0.22, 0.18)
    return jnp.clip(values, -limit, limit).astype(held_as)


def setup_inputs(seed: int = 0) -> dict:
    seeds = jax.random.split(jax.random.key(seed), 14)
    return {
        "tokens": scatter_about(seeds[0], (TOKENS, D), 1.0, 6.0, ((0, 32),)),
        "lengths": draw_lengths(jax.random.fold_in(seeds[13], 71), 0),
        "target": draw_target(jax.random.fold_in(seeds[13], 71), 0),
        "lang_group": draw_lang_group(jax.random.fold_in(seeds[13], 71), 0),
        "blocks": draw_blocks(jax.random.fold_in(seeds[13], 71), 0),
        "enc_gain": jnp.clip(1.0 + 0.1 * jax.random.normal(seeds[5], (D,), jnp.float32), 0.5, 1.5),
        "w_query": draw_w_query(jax.random.fold_in(seeds[13], 71), 0),
        "w_key": draw_w_key(jax.random.fold_in(seeds[13], 71), 0),
        "w_value": scatter_about(seeds[8], (D, HEADS * HDIM), D ** -0.5, 0.125, ((0, 2),)),
        "w_output": scatter_about(seeds[9], (HEADS * HDIM, D), (HEADS * HDIM) ** -0.5, 0.1875, ((0, 2),)),
        "moe_gain": jnp.clip(1.0 + 0.1 * jax.random.normal(seeds[10], (D,), jnp.float32), 0.5, 1.5),
        "expert_in": scatter_about(seeds[11], (EXPERTS, D, FF), D ** -0.5, 0.125, ((0, 16), (2, 2))),
        "expert_out": scatter_about(seeds[12], (EXPERTS, FF, D), FF ** -0.5, 0.09375, ((0, 16), (1, 2))),
    }


epsilon = 1e-05

def layer_norm(values, gain):
    floats = values.astype(jnp.float32)
    center = floats - lax.optimization_barrier(jnp.mean(floats, axis=-1, keepdims=True))
    spread = lax.optimization_barrier(jnp.mean(center * center, axis=-1, keepdims=True))
    return center * lax.rsqrt(spread + epsilon) * gain.astype(jnp.float32)

def sentence_ids(lengths, count):
    ends = jnp.cumsum(lengths)
    positions = jnp.arange(count, dtype=ends.dtype)
    return lax.optimization_barrier(jnp.sum((positions[:, None] >= ends[None, :]).astype(jnp.int32), axis=1))

def attend(query_rows, key_rows, value_rows, sentence):
    count = query_rows.shape[0]
    heads = query_rows.shape[1] // HDIM
    query_heads = query_rows.reshape(count, heads, HDIM)
    key_heads = key_rows.reshape(count, heads, HDIM)
    value_heads = value_rows.reshape(count, heads, HDIM)
    scores = jnp.einsum('qhd,khd->hqk', query_heads, key_heads, preferred_element_type=jnp.float32) / jnp.sqrt(jnp.float32(HDIM))
    same = sentence[:, None] == sentence[None, :]
    scores = jnp.where(same[None], scores, jnp.float32(-1e+30))
    top = lax.optimization_barrier(jnp.max(scores, axis=-1, keepdims=True))
    weights = jnp.exp(scores - top)
    probs = (weights / lax.optimization_barrier(jnp.sum(weights, axis=-1, keepdims=True))).astype(jnp.bfloat16)
    context = jnp.einsum('hqk,khd->qhd', probs, value_heads, preferred_element_type=jnp.float32)
    return context.astype(jnp.bfloat16).reshape(count, heads * HDIM)

def reference(tokens, lengths, target, lang_group, blocks, enc_gain, w_query, w_key, w_value, w_output, moe_gain, expert_in, expert_out):
    devices = N_LANG * N_FSDP
    total = tokens.shape[0]
    width = tokens.shape[1]
    normed = layer_norm(tokens, enc_gain).astype(jnp.bfloat16)
    query = jnp.dot(normed, w_query, preferred_element_type=jnp.float32).astype(jnp.bfloat16)
    keyed = jnp.dot(normed, w_key, preferred_element_type=jnp.float32).astype(jnp.bfloat16)
    valued = jnp.dot(normed, w_value, preferred_element_type=jnp.float32).astype(jnp.bfloat16)
    sent_dev = lengths.shape[0] // devices
    sentence = jax.vmap(lambda row: sentence_ids(row, TOK_DEV))(lengths.reshape(devices, sent_dev))

    def per_device(operands):
        return attend(operands[0], operands[1], operands[2], operands[3])
    context = lax.map(per_device, (query.reshape(devices, TOK_DEV, -1), keyed.reshape(devices, TOK_DEV, -1), valued.reshape(devices, TOK_DEV, -1), sentence))
    context = context.reshape(total, -1)
    hidden = (tokens.astype(jnp.float32) + jnp.dot(context, w_output, preferred_element_type=jnp.float32)).astype(jnp.bfloat16)
    routed = layer_norm(hidden, moe_gain).astype(jnp.bfloat16)
    sent_group = lang_group[target].astype(jnp.int32)
    tok_group = jnp.take_along_axis(sent_group.reshape(devices, sent_dev), sentence.astype(jnp.int32), axis=1).reshape(-1)
    device = (jnp.arange(total) // TOK_DEV).astype(jnp.int32)
    shard = device % N_FSDP
    bucket = (tok_group * N_FSDP + shard).astype(jnp.int32)
    order = jnp.argsort(bucket, stable=True).astype(jnp.int32)
    sorted_bucket = bucket[order]
    sizes = jnp.bincount(bucket, length=N_LANG * N_FSDP).astype(jnp.int32)
    starts = (jnp.cumsum(sizes) - sizes).astype(jnp.int32)
    within = jnp.arange(total).astype(jnp.int32) - starts[sorted_bucket]
    keep = within // BLOCK < blocks.reshape(-1)[sorted_bucket]
    span = N_FSDP * GCAP
    padded = jnp.concatenate([routed[order], jnp.zeros((span, width), jnp.bfloat16)], axis=0)
    group_start = starts[(jnp.arange(N_LANG) * N_FSDP).astype(jnp.int32)].astype(jnp.int32)

    def step(buffer, group):
        first = group_start[group].astype(jnp.int32)
        rows = lax.dynamic_slice_in_dim(padded, first, span, 0)
        inner = jax.nn.relu(jnp.dot(rows, expert_in[group], preferred_element_type=jnp.float32)).astype(jnp.bfloat16)
        result = jnp.dot(inner, expert_out[group], preferred_element_type=jnp.float32).astype(jnp.bfloat16)
        return (lax.dynamic_update_slice_in_dim(buffer, result, first, 0), None)
    filled = lax.scan(step, jnp.zeros_like(padded), jnp.arange(N_LANG).astype(jnp.int32))[0]
    expert_sorted = jnp.where(keep[:, None], filled[:total], jnp.zeros((), jnp.bfloat16))
    inverse = jnp.argsort(order).astype(jnp.int32)
    expert = expert_sorted[inverse]
    return (hidden.astype(jnp.float32) + expert.astype(jnp.float32)).astype(jnp.bfloat16)
```

```python
import functools

import jax
import jax.numpy as jnp
from jax import lax
from jax.experimental import pallas as pl
from jax.experimental.pallas import tpu as pltpu
from jax.sharding import PartitionSpec as P

HDIM = 128
BLOCK = 128
VMEM_LIMIT = 56 * 1024 * 1024

epsilon = 1e-05


def layer_norm(values, gain):
    floats = values.astype(jnp.float32)
    center = floats - jnp.mean(floats, axis=-1, keepdims=True)
    spread = jnp.mean(center * center, axis=-1, keepdims=True)
    return center * lax.rsqrt(spread + epsilon) * gain


def attend(query_rows, key_rows, value_rows, sentence):
    count = query_rows.shape[0]
    heads = query_rows.shape[1] // HDIM
    query_heads = query_rows.reshape(count, heads, HDIM)
    key_heads = key_rows.reshape(count, heads, HDIM)
    value_heads = value_rows.reshape(count, heads, HDIM)
    scores = jnp.einsum(
        "qhd,khd->hqk", query_heads, key_heads, preferred_element_type=jnp.float32
    ) / jnp.sqrt(jnp.float32(HDIM))
    same = sentence[:, None] == sentence[None, :]
    scores = jnp.where(same[None], scores, jnp.float32(-1e30))
    top = jnp.max(scores, axis=-1, keepdims=True)
    weights = jnp.exp(scores - top)
    probs = (weights / jnp.sum(weights, axis=-1, keepdims=True)).astype(jnp.bfloat16)
    context = jnp.einsum("hqk,khd->qhd", probs, value_heads, preferred_element_type=jnp.float32)
    return context.astype(jnp.bfloat16).reshape(count, heads * HDIM)


def expert_kernel(slots, rows, pieces, per, *refs):
    ins = refs[:slots]
    first = refs[slots : slots + pieces]
    second = refs[slots + pieces : slots + 2 * pieces]
    outs = refs[slots + 2 * pieces : 2 * slots + 2 * pieces]
    packed, total = refs[2 * slots + 2 * pieces :]
    step = pl.program_id(0)

    @pl.when(step == 0)
    def _():
        for s in range(slots):
            packed[s * rows : (s + 1) * rows, :] = ins[s][...]
        total[...] = jnp.zeros_like(total)

    for p in range(pieces):

        @pl.when(step // per == p)
        def _():
            inner = jnp.dot(packed[...], first[p][...], preferred_element_type=jnp.float32)
            inner = jnp.maximum(inner, 0.0).astype(jnp.bfloat16)
            total[...] += jnp.dot(inner, second[p][...], preferred_element_type=jnp.float32)

    @pl.when(step == pieces * per - 1)
    def _():
        for s in range(slots):
            outs[s][...] = total[s * rows : (s + 1) * rows, :].astype(jnp.bfloat16)


def expert_ffn(ins, first, second):
    slots, pieces = len(ins), len(first)
    rows, width = ins[0].shape
    hidden = first[0].shape[1]
    chunk = 512 if hidden % 512 == 0 else hidden
    per = hidden // chunk

    def at(p, i):
        return jnp.clip(i - p * per, 0, per - 1)

    whole = pl.BlockSpec((rows, width), lambda i: (0, 0))
    return pl.pallas_call(
        functools.partial(expert_kernel, slots, rows, pieces, per),
        grid=(pieces * per,),
        in_specs=[whole] * slots
        + [pl.BlockSpec((width, chunk), lambda i, p=p: (0, at(p, i))) for p in range(pieces)]
        + [pl.BlockSpec((chunk, width), lambda i, p=p: (at(p, i), 0)) for p in range(pieces)],
        out_specs=[whole] * slots,
        out_shape=[jax.ShapeDtypeStruct((rows, width), jnp.bfloat16)] * slots,
        scratch_shapes=[
            pltpu.VMEM((slots * rows, width), jnp.bfloat16),
            pltpu.VMEM((slots * rows, width), jnp.float32),
        ],
        compiler_params=pltpu.CompilerParams(
            dimension_semantics=("arbitrary",), vmem_limit_bytes=VMEM_LIMIT
        ),
    )(*ins, *first, *second)


def body(
    tokens,
    lengths,
    target,
    lang_group,
    blocks,
    enc_gain,
    w_query,
    w_key,
    w_value,
    w_output,
    moe_gain,
    expert_in,
    expert_out,
):
    count, width = tokens.shape
    lang_count, fsdp_count = lax.axis_size("lang"), lax.axis_size("fsdp")
    lang_at, fsdp_at = lax.axis_index("lang"), lax.axis_index("fsdp")
    slots_dev = min(32, lang_count // 2)
    capacity = count // slots_dev

    def pieces_of(shard):
        return [shard] + [
            lax.ppermute(shard, "fsdp", [(i, (i + s) % fsdp_count) for i in range(fsdp_count)])
            for s in range(1, fsdp_count)
        ]

    def columns_of(rows):
        part = rows.shape[1] // fsdp_count
        return [
            lax.dynamic_slice_in_dim(rows, (fsdp_at - s) % fsdp_count * part, part, 1)
            for s in range(fsdp_count)
        ]

    def product(columns, pieces):
        return sum(
            jnp.dot(c, w, preferred_element_type=jnp.float32) for c, w in zip(columns, pieces)
        )

    query_w, key_w, value_w, output_w = map(pieces_of, (w_query, w_key, w_value, w_output))

    ends = jnp.cumsum(lengths)
    positions = jnp.arange(count, dtype=jnp.int32)
    sentence = jnp.sum((positions[:, None] >= ends[None, :]).astype(jnp.int32), axis=1)
    lang_ids = jnp.arange(lang_group.shape[0], dtype=jnp.int32)
    sent_group = jnp.sum(
        jnp.where(target[:, None] == lang_ids[None, :], lang_group[None, :], 0), axis=1
    )
    run_ids = jnp.arange(slots_dev, dtype=jnp.int32)
    run_sent = jnp.sum((run_ids[:, None] * capacity >= ends[None, :]).astype(jnp.int32), axis=1)
    sent_ids = jnp.arange(lengths.shape[0], dtype=jnp.int32)
    run_group = jnp.sum(
        jnp.where(run_sent[:, None] == sent_ids[None, :], sent_group[None, :], 0), axis=1
    )
    group_ids = jnp.arange(lang_count, dtype=jnp.int32)
    sends = jnp.any(run_group[:, None] == group_ids[None, :], axis=0).astype(jnp.int32)
    mine = group_ids[:, None] == lang_at
    table = lax.psum(
        jnp.concatenate(
            [jnp.where(mine, sends[None, :], 0), jnp.where(mine, blocks[:, :1], 0)], axis=1
        ),
        "lang",
    )
    before = jnp.sum(jnp.where(group_ids[:, None] < lang_at, table[:, :lang_count], 0), axis=0)
    group_live = before * capacity // BLOCK < table[:, lang_count]
    run_live = jnp.any((run_group[:, None] == group_ids[None, :]) & group_live[None, :], axis=1)

    normed = layer_norm(tokens, enc_gain).astype(jnp.bfloat16)
    columns = columns_of(normed)
    query = product(columns, query_w).astype(jnp.bfloat16)
    keyed = product(columns, key_w).astype(jnp.bfloat16)
    valued = product(columns, value_w).astype(jnp.bfloat16)
    context = attend(query, keyed, valued, sentence)
    attention = product(columns_of(context), output_w)
    hidden = (tokens.astype(jnp.float32) + attention).astype(jnp.bfloat16)
    routed = layer_norm(hidden, moe_gain).astype(jnp.bfloat16)

    dispatch = (group_ids[:, None] == run_group[None, :]).astype(jnp.bfloat16)
    runs = routed.reshape(slots_dev, capacity * width)
    outgoing = jnp.dot(dispatch, runs, preferred_element_type=jnp.float32).astype(jnp.bfloat16)
    incoming = lax.all_to_all(
        outgoing.reshape(lang_count, capacity, width), "lang", 0, 0, tiled=True
    )
    expert_shards = lax.optimization_barrier((expert_in[0], expert_out[0], *output_w))[:2]
    first, second = map(pieces_of, expert_shards)
    (result,) = expert_ffn([incoming.reshape(lang_count * capacity, width)], first, second)
    back = lax.all_to_all(result.reshape(lang_count, capacity, width), "lang", 0, 0, tiled=True)
    expert = jnp.dot(
        (dispatch * run_live[None, :].astype(jnp.bfloat16)).T,
        back.reshape(lang_count, capacity * width),
        preferred_element_type=jnp.float32,
    ).reshape(count, width)
    return (hidden.astype(jnp.float32) + expert).astype(jnp.bfloat16)


def solution(mesh):
    return jax.shard_map(
        body,
        mesh=mesh,
        in_specs=(
            P(("lang", "fsdp"), None),
            P(("lang", "fsdp")),
            P(("lang", "fsdp")),
            P(),
            P("lang", "fsdp"),
            P(),
            P("fsdp", None),
            P("fsdp", None),
            P("fsdp", None),
            P("fsdp", None),
            P(),
            P("lang", None, "fsdp"),
            P("lang", "fsdp", None),
        ),
        out_specs=P(("lang", "fsdp"), None),
        check_vma=False,
    )
```

```python
import functools

import jax
import jax.numpy as jnp
from jax import lax
from jax.experimental import pallas as pl
from jax.experimental.pallas import tpu as pltpu
from jax.sharding import PartitionSpec as P

HDIM = 128
BLOCK = 128
VMEM_LIMIT = 60 * 1024 * 1024
FRONT_LIMIT = 24 * 1024 * 1024

epsilon = 1e-05


def layer_norm(values, gain):
    floats = values.astype(jnp.float32)
    center = floats - jnp.mean(floats, axis=-1, keepdims=True)
    spread = jnp.mean(center * center, axis=-1, keepdims=True)
    return center * lax.rsqrt(spread + epsilon) * gain


def dot(a, b):
    return jnp.dot(a, b, preferred_element_type=jnp.float32)


def in_vmem(count):
    return [pl.BlockSpec(memory_space=pltpu.VMEM)] * count


def cost(macs, *arrays):
    size = sum(a.size * a.dtype.itemsize for a in arrays)
    return pl.CostEstimate(flops=2 * macs, bytes_accessed=size, transcendentals=0)


def project_kernel(pieces, at_ref, tokens, gain, *refs):
    weights, rest, sums = refs[:3], refs[3 : 2 + pieces], refs[2 + pieces : 5 + pieces]
    own = refs[-1]
    part = own.shape[1]
    normed = layer_norm(tokens[...], gain[...]).astype(jnp.bfloat16)
    for v in range(pieces):

        @pl.when(at_ref[0] == v)
        def _():
            for s, ref in enumerate((own, *rest)):
                first = (v - s) % pieces * part
                ref[...] = normed[:, first : first + part]

    for weight, total in zip(weights, sums):
        total[...] = dot(own[...], weight[...])


def project(at, tokens, gain, weights, pieces):
    count, width = tokens.shape
    part, wide = weights[0].shape
    out = pl.pallas_call(
        functools.partial(project_kernel, pieces),
        in_specs=[pl.BlockSpec(memory_space=pltpu.SMEM)] + in_vmem(5),
        out_specs=in_vmem(pieces + 2),
        out_shape=[jax.ShapeDtypeStruct((count, part), jnp.bfloat16)] * (pieces - 1)
        + [jax.ShapeDtypeStruct((count, wide), jnp.float32)] * 3,
        scratch_shapes=[pltpu.VMEM((count, part), jnp.bfloat16)],
        compiler_params=pltpu.CompilerParams(vmem_limit_bytes=FRONT_LIMIT),
        cost_estimate=cost(3 * count * part * wide, tokens, *weights),
    )(at, tokens, gain, *weights)
    return out[: pieces - 1], out[pieces - 1 :]


def attend_kernel(rest_count, bias, *refs):
    rest = refs[:rest_count]
    sums = refs[rest_count : rest_count + 3]
    weights = refs[rest_count + 3 : -2]
    context, scores = refs[-2:]

    def full(n):
        total = sums[n][...]
        for s in range(rest_count):
            total += dot(rest[s][...], weights[n * rest_count + s][...])
        return total.astype(jnp.bfloat16)

    count, block = bias.shape
    query, keyed = full(0), full(1)
    heads = query.shape[1] // HDIM
    tiles = [
        (h, slice(h * HDIM, (h + 1) * HDIM), slice(top, top + block))
        for h in range(heads)
        for top in range(0, count, block)
    ]
    for h, head, rows in tiles:
        product = lax.dot_general(
            query[rows, head], keyed[rows, head], (((1,), (1,)), ((), ())),
            preferred_element_type=jnp.float32,
        )
        scores[h, rows, :] = product * (HDIM**-0.5) + bias[rows, :]
    valued = full(2)
    for h, head, rows in tiles:
        tile = scores[h, rows, :]
        weight = jnp.exp(tile - jnp.max(tile, axis=-1, keepdims=True))
        probs = (weight / jnp.sum(weight, axis=-1, keepdims=True)).astype(jnp.bfloat16)
        context[rows, head] = dot(probs, valued[rows, head]).astype(jnp.bfloat16)


def attend(bias, rest, sums, weights):
    count, wide = sums[0].shape
    flat = [w for pieces in weights for w in pieces]
    return pl.pallas_call(
        functools.partial(attend_kernel, len(rest)),
        in_specs=in_vmem(4 + len(rest) + len(flat)),
        out_specs=in_vmem(1)[0],
        out_shape=jax.ShapeDtypeStruct((count, wide), jnp.bfloat16),
        scratch_shapes=[pltpu.VMEM((wide // HDIM, *bias.shape), jnp.float32)],
        compiler_params=pltpu.CompilerParams(vmem_limit_bytes=FRONT_LIMIT),
        cost_estimate=cost(2 * count * sum(w.size for w in flat), *flat, *sums),
    )(bias, *rest, *sums, *flat)


def hidden_kernel(pieces, runs, slots, at_ref, run_ref, context, tokens, gain, *refs):
    weights, hidden, outs, routed = refs[:pieces], refs[pieces], refs[pieces + 1 : -1], refs[-1]
    part = weights[0].shape[0]
    count = tokens.shape[0]
    total = tokens[...].astype(jnp.float32)
    for s in range(pieces):
        first = lax.rem(at_ref[0] + pieces - s, pieces) * part
        total += dot(context[:, pl.ds(pl.multiple_of(first, 128), part)], weights[s][...])
    hidden[...] = total.astype(jnp.bfloat16)
    rows = count // runs
    for j in range(runs):
        run = slice(j * rows, (j + 1) * rows)
        normed = layer_norm(hidden[run, :], gain[...]).astype(jnp.bfloat16)
        if slots:
            routed[j] = normed
        else:
            outs[0][run, :] = normed
    if slots:
        routed[runs] = jnp.zeros_like(routed[runs])
        for k in range(slots):
            outs[k][...] = routed[run_ref[k]]


def hidden_states(at, run_of_slot, context, tokens, gain, weights, runs, slots):
    count, width = tokens.shape
    rows = count // runs
    outs = [(rows, width)] * slots if slots else [(count, width)]
    out = pl.pallas_call(
        functools.partial(hidden_kernel, len(weights), runs, slots),
        in_specs=[pl.BlockSpec(memory_space=pltpu.SMEM)] * 2 + in_vmem(3 + len(weights)),
        out_specs=in_vmem(1 + len(outs)),
        out_shape=[
            jax.ShapeDtypeStruct(shape, jnp.bfloat16) for shape in [tokens.shape, *outs]
        ],
        scratch_shapes=[pltpu.VMEM((runs + 1, rows, width), jnp.bfloat16)],
        compiler_params=pltpu.CompilerParams(vmem_limit_bytes=FRONT_LIMIT),
        cost_estimate=cost(context.size * width, context, tokens, *weights),
    )(at, run_of_slot, context, tokens, gain, *weights)
    return out[0], out[1:]


def mix_kernel(slots, runs, run_ref, live_ref, hidden, *refs):
    ins, mixed = refs[:slots], refs[slots]
    rows = hidden.shape[0] // runs
    for k in range(slots):

        @pl.when(run_ref[k] < runs)
        def _():
            run = pl.ds(pl.multiple_of(run_ref[k] * rows, rows), rows)
            expert = jnp.where(live_ref[k] > 0, ins[k][...].astype(jnp.float32), 0.0)
            mixed[run, :] = (hidden[run, :].astype(jnp.float32) + expert).astype(jnp.bfloat16)


def mix(run_of_slot, slot_live, hidden, ins, runs):
    return pl.pallas_call(
        functools.partial(mix_kernel, len(ins), runs),
        in_specs=[pl.BlockSpec(memory_space=pltpu.SMEM)] * 2
        + [pl.BlockSpec(memory_space=pltpu.VMEM)] * (1 + len(ins)),
        out_specs=pl.BlockSpec(memory_space=pltpu.VMEM),
        out_shape=jax.ShapeDtypeStruct(hidden.shape, jnp.bfloat16),
        compiler_params=pltpu.CompilerParams(vmem_limit_bytes=FRONT_LIMIT),
    )(run_of_slot, slot_live, hidden, *ins)


def expert_kernel(slots, rows, pieces, per, *refs):
    ins = refs[:slots]
    first = refs[slots : slots + pieces]
    second = refs[slots + pieces : slots + 2 * pieces]
    outs = refs[slots + 2 * pieces : 2 * slots + 2 * pieces]
    packed, total = refs[2 * slots + 2 * pieces :]
    step = pl.program_id(0)

    @pl.when(step == 0)
    def _():
        for s in range(slots):
            packed[s * rows : (s + 1) * rows, :] = ins[s][...]
        total[...] = jnp.zeros_like(total)

    for p in range(pieces):

        @pl.when(step // per == p)
        def _():
            inner = jnp.dot(packed[...], first[p][...], preferred_element_type=jnp.float32)
            inner = jnp.maximum(inner, 0.0).astype(jnp.bfloat16)
            total[...] += jnp.dot(inner, second[p][...], preferred_element_type=jnp.float32)

    @pl.when(step == pieces * per - 1)
    def _():
        for s in range(slots):
            outs[s][...] = total[s * rows : (s + 1) * rows, :].astype(jnp.bfloat16)


def expert_ffn(ins, first, second):
    slots, pieces = len(ins), len(first)
    rows, width = ins[0].shape
    hidden = first[0].shape[1]
    chunk = 512 if hidden % 512 == 0 else hidden
    per = hidden // chunk

    def at(p, i):
        return jnp.clip(i - p * per, 0, per - 1)

    whole = pl.BlockSpec((rows, width), lambda i: (0, 0))
    return pl.pallas_call(
        functools.partial(expert_kernel, slots, rows, pieces, per),
        grid=(pieces * per,),
        in_specs=[whole] * slots
        + [pl.BlockSpec((width, chunk), lambda i, p=p: (0, at(p, i))) for p in range(pieces)]
        + [pl.BlockSpec((chunk, width), lambda i, p=p: (at(p, i), 0)) for p in range(pieces)],
        out_specs=[whole] * slots,
        out_shape=[jax.ShapeDtypeStruct((rows, width), jnp.bfloat16)] * slots,
        scratch_shapes=[
            pltpu.VMEM((slots * rows, width), jnp.bfloat16),
            pltpu.VMEM((slots * rows, width), jnp.float32),
        ],
        compiler_params=pltpu.CompilerParams(
            dimension_semantics=("arbitrary",), vmem_limit_bytes=VMEM_LIMIT
        ),
        cost_estimate=cost(2 * slots * rows * width * hidden * pieces, *first, *second),
    )(*ins, *first, *second)


def body(
    tokens,
    lengths,
    target,
    lang_group,
    blocks,
    enc_gain,
    w_query,
    w_key,
    w_value,
    w_output,
    moe_gain,
    expert_in,
    expert_out,
):
    count, width = tokens.shape
    lang_count, fsdp_count = lax.axis_size("lang"), lax.axis_size("fsdp")
    lang_at, fsdp_at = lax.axis_index("lang"), lax.axis_index("fsdp")
    slots_dev = min(32, lang_count // 2)
    capacity = count // slots_dev
    direct = lang_count <= 16 and lang_count & (lang_count - 1) == 0 and capacity % 16 == 0
    fsdp_scalar = fsdp_at.astype(jnp.int32).reshape(1)

    def others(shard):
        return [
            lax.ppermute(shard, "fsdp", [(i, (i + s) % fsdp_count) for i in range(fsdp_count)])
            for s in range(1, fsdp_count)
        ]

    ends = jnp.cumsum(lengths)
    positions = jnp.arange(count, dtype=jnp.int32)
    sentence = jnp.sum((positions[:, None] >= ends[None, :]).astype(jnp.int32), axis=1)
    lang_ids = jnp.arange(lang_group.shape[0], dtype=jnp.int32)
    sent_group = jnp.sum(
        jnp.where(target[:, None] == lang_ids[None, :], lang_group[None, :], 0), axis=1
    )
    run_ids = jnp.arange(slots_dev, dtype=jnp.int32)
    run_sent = jnp.sum((run_ids[:, None] * capacity >= ends[None, :]).astype(jnp.int32), axis=1)
    sent_ids = jnp.arange(lengths.shape[0], dtype=jnp.int32)
    run_group = jnp.sum(
        jnp.where(run_sent[:, None] == sent_ids[None, :], sent_group[None, :], 0), axis=1
    )
    group_ids = jnp.arange(lang_count, dtype=jnp.int32)
    sends = jnp.any(run_group[:, None] == group_ids[None, :], axis=0).astype(jnp.int32)
    mine = group_ids[:, None] == lang_at
    table = jnp.concatenate(
        [jnp.where(mine, sends[None, :], 0), jnp.where(mine, blocks[:, :1], 0)], axis=1
    )
    step = 1
    while step < lang_count:
        table += lax.ppermute(table, "lang", [(i, i ^ step) for i in range(lang_count)])
        step *= 2
    before = jnp.sum(jnp.where(group_ids[:, None] < lang_at, table[:, :lang_count], 0), axis=0)
    group_live = before * capacity // BLOCK < table[:, lang_count]
    slot_group = jnp.bitwise_xor(group_ids, lang_at.astype(jnp.int32))
    run_of_slot = slots_dev - jnp.sum(
        jnp.where(run_group[None, :] == slot_group[:, None], slots_dev - run_ids[None, :], 0),
        axis=1,
    )
    slot_live = jnp.any(
        (slot_group[:, None] == group_ids[None, :]) & group_live[None, :], axis=1
    ).astype(jnp.int32)

    weights = (w_query, w_key, w_value)
    later = [others(w) for w in weights]
    rest, sums = project(fsdp_scalar, tokens, enc_gain[None, :], weights, fsdp_count)
    block = 128 if count % 128 == 0 and 128 % capacity == 0 else count
    keys = sentence.reshape(count // block, 1, block)
    same = sentence.reshape(count // block, block, 1) == keys
    bias = jnp.where(same, jnp.float32(0), jnp.float32(-1e30)).reshape(count, block)
    bias, run_of_slot, slot_live, w_output, later = lax.optimization_barrier(
        (bias, run_of_slot, slot_live, w_output, later)
    )
    output_w = [w_output, *others(w_output)]
    context = attend(bias, rest, sums, later)
    context, output_w, *shards = lax.optimization_barrier(
        (context, output_w, expert_in[0], expert_out[0])
    )
    first, second = ([shard, *others(shard)] for shard in shards)
    hidden, slots = hidden_states(
        fsdp_scalar, run_of_slot, context, tokens, moe_gain[None, :], output_w, slots_dev,
        lang_count if direct else 0,
    )

    def swap(ks, arrays):
        return [
            lax.ppermute(a, "lang", [(i, i ^ k) for i in range(lang_count)])
            for k, a in zip(ks, arrays)
        ]

    if direct:
        half, quarter = lang_count // 2, lang_count // 4
        near = list(range(1, half))
        far = list(range(half, half + quarter))
        last = list(range(half + quarter, lang_count))

        def after(arrays, *done):
            return list(lax.optimization_barrier((tuple(arrays), done))[0])

        far_in = swap(far, [slots[k] for k in far])
        near_in = swap(near, [slots[k] for k in near])
        last_in = []
        for n, k in enumerate(last):
            last_in += swap([k], after([slots[k]], far_in[min(n + 1, quarter - 2)]))
        far_out = expert_ffn(after(far_in, near_in), first, second)
        far_back = swap(far, far_out)
        out = expert_ffn(after([slots[0], *near_in, *last_in], far_out), first, second)
        last_back = swap(last, after(out[half:], far_back))
        near_back = swap(near, after(out[1:half], last_back[0]))
        back = [out[0], *near_back, *far_back, *last_back]
        return mix(run_of_slot, slot_live, hidden, back, slots_dev)

    dispatch = (group_ids[:, None] == run_group[None, :]).astype(jnp.bfloat16)
    runs = slots[0].reshape(slots_dev, capacity * width)
    outgoing = jnp.dot(dispatch, runs, preferred_element_type=jnp.float32).astype(jnp.bfloat16)
    incoming = lax.all_to_all(
        outgoing.reshape(lang_count, capacity, width), "lang", 0, 0, tiled=True
    )
    (result,) = expert_ffn([incoming.reshape(lang_count * capacity, width)], first, second)
    back = lax.all_to_all(result.reshape(lang_count, capacity, width), "lang", 0, 0, tiled=True)
    expert = lax.dot_general(
        dispatch * group_live[:, None].astype(jnp.bfloat16),
        back.reshape(lang_count, capacity * width),
        (((0,), (0,)), ((), ())),
        preferred_element_type=jnp.float32,
    ).reshape(count, width)
    return (hidden.astype(jnp.float32) + expert).astype(jnp.bfloat16)


def solution(mesh):
    return jax.shard_map(
        body,
        mesh=mesh,
        in_specs=(
            P(("lang", "fsdp"), None),
            P(("lang", "fsdp")),
            P(("lang", "fsdp")),
            P(),
            P("lang", "fsdp"),
            P(),
            P("fsdp", None),
            P("fsdp", None),
            P("fsdp", None),
            P("fsdp", None),
            P(),
            P("lang", None, "fsdp"),
            P("lang", "fsdp", None),
        ),
        out_specs=P(("lang", "fsdp"), None),
        check_vma=False,
    )
```

```python
import functools

import jax
import jax.numpy as jnp
from jax import lax
from jax.experimental import pallas as pl
from jax.experimental.pallas import tpu as pltpu
from jax.sharding import PartitionSpec as P

HDIM = 128
BLOCK = 128
VMEM_LIMIT = 30 * 1024 * 1024
FRONT_LIMIT = 24 * 1024 * 1024

EMPTY = 1024.0

epsilon = 1e-05


def layer_norm(values, gain):
    floats = values.astype(jnp.float32)
    center = floats - jnp.mean(floats, axis=-1, keepdims=True)
    spread = jnp.mean(center * center, axis=-1, keepdims=True)
    return center * lax.rsqrt(spread + epsilon) * gain


def dot(a, b):
    return jnp.dot(a, b, preferred_element_type=jnp.float32)


def in_vmem(count):
    return [pl.BlockSpec(memory_space=pltpu.VMEM)] * count


def cost(macs, *arrays):
    size = sum(a.size * a.dtype.itemsize for a in arrays)
    return pl.CostEstimate(flops=2 * macs, bytes_accessed=size, transcendentals=0)


def project_kernel(pieces, at_ref, tokens, gain, *refs):
    weights, rest, sums = refs[:3], refs[3 : 2 + pieces], refs[2 + pieces : 5 + pieces]
    own, held, arrived = refs[-3:]
    part = own.shape[1]
    copies = [
        pltpu.make_async_copy(weight, held.at[n], arrived.at[n]) for n, weight in enumerate(weights)
    ]
    for copy in copies:
        copy.start()
    normed = layer_norm(tokens[...], gain[...]).astype(jnp.bfloat16)
    for v in range(pieces):

        @pl.when(at_ref[0] == v)
        def _():
            for s, ref in enumerate((own, *rest)):
                first = (v - s) % pieces * part
                ref[...] = normed[:, first : first + part]

    for n, total in enumerate(sums):
        copies[n].wait()
        total[...] = dot(own[...], held[n])


def project(at, tokens, gain, weights, pieces):
    count, width = tokens.shape
    part, wide = weights[0].shape
    out = pl.pallas_call(
        functools.partial(project_kernel, pieces),
        in_specs=[pl.BlockSpec(memory_space=pltpu.SMEM)]
        + in_vmem(2)
        + [pl.BlockSpec(memory_space=pltpu.HBM)] * 3,
        out_specs=in_vmem(pieces + 2),
        out_shape=[jax.ShapeDtypeStruct((count, part), jnp.bfloat16)] * (pieces - 1)
        + [jax.ShapeDtypeStruct((count, wide), jnp.float32)] * 3,
        scratch_shapes=[
            pltpu.VMEM((count, part), jnp.bfloat16),
            pltpu.VMEM((3, part, wide), jnp.bfloat16),
            pltpu.SemaphoreType.DMA((3,)),
        ],
        compiler_params=pltpu.CompilerParams(vmem_limit_bytes=FRONT_LIMIT),
        cost_estimate=cost(3 * count * part * wide, tokens, *weights),
    )(at, tokens, gain, *weights)
    return out[: pieces - 1], out[pieces - 1 :]


def attend_kernel(rest_count, bias, *refs):
    rest = refs[:rest_count]
    sums = refs[rest_count : rest_count + 3]
    weights = refs[rest_count + 3 : -2]
    context, scores = refs[-2:]

    def full(n):
        total = sums[n][...]
        for s in range(rest_count):
            total += dot(rest[s][...], weights[n * rest_count + s][...])
        return total.astype(jnp.bfloat16)

    count, block = bias.shape
    query, keyed = full(0), full(1)
    heads = query.shape[1] // HDIM
    tiles = [
        (h, slice(h * HDIM, (h + 1) * HDIM), slice(top, top + block))
        for h in range(heads)
        for top in range(0, count, block)
    ]
    for h, head, rows in tiles:
        product = lax.dot_general(
            query[rows, head], keyed[rows, head], (((1,), (1,)), ((), ())),
            preferred_element_type=jnp.float32,
        )
        scores[h, rows, :] = product * (HDIM**-0.5) + bias[rows, :]
    valued = full(2)
    for h, head, rows in tiles:
        tile = scores[h, rows, :]
        weight = jnp.exp(tile - jnp.max(tile, axis=-1, keepdims=True))
        probs = (weight / jnp.sum(weight, axis=-1, keepdims=True)).astype(jnp.bfloat16)
        context[rows, head] = dot(probs, valued[rows, head]).astype(jnp.bfloat16)


def attend(bias, rest, sums, weights):
    count, wide = sums[0].shape
    flat = [w for pieces in weights for w in pieces]
    return pl.pallas_call(
        functools.partial(attend_kernel, len(rest)),
        in_specs=in_vmem(4 + len(rest) + len(flat)),
        out_specs=in_vmem(1)[0],
        out_shape=jax.ShapeDtypeStruct((count, wide), jnp.bfloat16),
        scratch_shapes=[pltpu.VMEM((wide // HDIM, *bias.shape), jnp.float32)],
        compiler_params=pltpu.CompilerParams(vmem_limit_bytes=FRONT_LIMIT),
        cost_estimate=cost(2 * count * sum(w.size for w in flat), *flat, *sums),
    )(bias, *rest, *sums, *flat)


def hidden_kernel(pieces, runs, slots, at_ref, run_ref, context, tokens, gain, *refs):
    weights, hidden, outs, routed = refs[:pieces], refs[pieces], refs[pieces + 1 : -1], refs[-1]
    part = weights[0].shape[0]
    count = tokens.shape[0]
    total = tokens[...].astype(jnp.float32)
    for s in range(pieces):
        first = lax.rem(at_ref[0] + pieces - s, pieces) * part
        total += dot(context[:, pl.ds(pl.multiple_of(first, 128), part)], weights[s][...])
    hidden[...] = total.astype(jnp.bfloat16)
    rows = count // runs
    for j in range(runs):
        run = slice(j * rows, (j + 1) * rows)
        normed = layer_norm(hidden[run, :], gain[...]).astype(jnp.bfloat16)
        if slots:
            routed[j] = normed
        else:
            outs[0][run, :] = normed
    if slots:
        routed[runs] = jnp.full_like(routed[runs], EMPTY)
        near = outs[0].shape[0]
        for k in range(slots):
            if k < near:
                outs[0][k] = routed[run_ref[k]]
            else:
                outs[1 + k - near][...] = routed[run_ref[k]]


def hidden_states(at, run_of_slot, context, tokens, gain, weights, runs, slots):
    count, width = tokens.shape
    rows = count // runs
    near = slots // 2
    outs = [(near, rows, width)] + [(rows, width)] * near if slots else [(count, width)]
    out = pl.pallas_call(
        functools.partial(hidden_kernel, len(weights), runs, slots),
        in_specs=[pl.BlockSpec(memory_space=pltpu.SMEM)] * 2 + in_vmem(3 + len(weights)),
        out_specs=in_vmem(1 + len(outs)),
        out_shape=[
            jax.ShapeDtypeStruct(shape, jnp.bfloat16) for shape in [tokens.shape, *outs]
        ],
        scratch_shapes=[pltpu.VMEM((runs + 1, rows, width), jnp.bfloat16)],
        compiler_params=pltpu.CompilerParams(vmem_limit_bytes=FRONT_LIMIT),
        cost_estimate=cost(context.size * width, context, tokens, *weights),
    )(at, run_of_slot, context, tokens, gain, *weights)
    return out[0], out[1:]


def mix_kernel(runs, run_ref, hidden, near, *refs):
    far, mixed = refs[:-1], refs[-1]
    rows = hidden.shape[0] // runs
    half = near.shape[0]
    for k in range(half + len(far)):

        @pl.when(run_ref[k] < runs)
        def _():
            run = pl.ds(pl.multiple_of(run_ref[k] * rows, rows), rows)
            expert = near[k] if k < half else far[k - half][...]
            total = hidden[run, :].astype(jnp.float32) + expert.astype(jnp.float32)
            mixed[run, :] = total.astype(jnp.bfloat16)


def mix(run_of_slot, hidden, near, far, runs):
    return pl.pallas_call(
        functools.partial(mix_kernel, runs),
        in_specs=[pl.BlockSpec(memory_space=pltpu.SMEM)] + in_vmem(2 + len(far)),
        out_specs=in_vmem(1)[0],
        out_shape=jax.ShapeDtypeStruct(hidden.shape, jnp.bfloat16),
        compiler_params=pltpu.CompilerParams(vmem_limit_bytes=FRONT_LIMIT),
    )(run_of_slot, hidden, near, *far)


def live_kernel(first, at_ref, blocks_ref, near, *refs):
    count = (len(refs) - 1 - 2 * first)
    far, results, outs, live = refs[:count], refs[count : count + first], refs[-1 - first : -1], refs[-1]
    half, rows = near.shape[:2]
    me = at_ref[0]
    heads = [near[k, :16, :128] for k in range(half)] + [ref[:16, :128] for ref in far]
    full = [(jnp.max(head.astype(jnp.float32)) < EMPTY / 2).astype(jnp.int32) for head in heads]
    source = [me // half * half + k for k in range(half)]
    source += [jnp.bitwise_xor(me, half + k) for k in range(len(far))]
    for k in range(half + len(far)):
        before = sum(jnp.where(s < source[k], f, 0) for s, f in zip(source, full))
        live[k] = (before * rows // BLOCK < blocks_ref[0, 0]).astype(jnp.int32)
    for k in range(first):
        kept = live[half + k] > 0
        outs[k][...] = jnp.where(kept, results[k][...], jnp.zeros_like(results[k]))


def live_rows(at, blocks, near, far, results):
    first = len(results)
    smem = pl.BlockSpec(memory_space=pltpu.SMEM)
    out = pl.pallas_call(
        functools.partial(live_kernel, first),
        in_specs=[smem] * 2 + in_vmem(1 + len(far) + first),
        out_specs=in_vmem(first) + [smem],
        out_shape=[jax.ShapeDtypeStruct(r.shape, r.dtype) for r in results]
        + [jax.ShapeDtypeStruct((near.shape[0] + len(far),), jnp.int32)],
        compiler_params=pltpu.CompilerParams(vmem_limit_bytes=FRONT_LIMIT),
    )(at, blocks, near, *far, *results)
    return out[:first], out[first]


def expert_kernel(sizes, pieces, per, slots, live, *refs):
    count = len(sizes)
    ins, outs = refs[:count], refs[count + 2 * pieces : 2 * count + 2 * pieces]
    first, second = refs[count : count + pieces], refs[count + pieces : count + 2 * pieces]
    packed, total = refs[-2:]
    step = pl.program_id(0)
    tops = [sum(sizes[:n]) for n in range(count)]

    @pl.when(step == 0)
    def _():
        for top, size, ref in zip(tops, sizes, ins):
            packed[top : top + size, :] = ref[...]
        total[...] = jnp.zeros_like(total)

    for p in range(pieces):

        @pl.when(step // per == p)
        def _():
            inner = jnp.maximum(dot(packed[...], first[p][...]), 0.0).astype(jnp.bfloat16)
            total[...] += dot(inner, second[p][...])

    @pl.when(step == pieces * per - 1)
    def _():
        for n, (top, size, ref) in enumerate(zip(tops, sizes, outs)):
            rows = size // max(1, len(slots[n]))
            for m, slot in enumerate(slots[n]):
                part = slice(top + m * rows, top + (m + 1) * rows)
                kept = jnp.where(live[slot] > 0, total[part, :], 0.0)
                ref[m * rows : (m + 1) * rows, :] = kept.astype(jnp.bfloat16)
            if not slots[n]:
                ref[...] = total[top : top + size, :].astype(jnp.bfloat16)


def expert_ffn(ins, first, second, live=None, slots=None):
    pieces, (width, hidden) = len(first), first[0].shape
    sizes = [a.shape[0] for a in ins]
    rows = sum(sizes)
    chunk = 512 if hidden % 512 == 0 else hidden
    per = hidden // chunk
    if live is None:
        live, slots = jnp.zeros((1,), jnp.int32), [[]] * len(ins)

    def at(p, i):
        return jnp.clip(i - p * per, 0, per - 1)

    return pl.pallas_call(
        functools.partial(expert_kernel, sizes, pieces, per, slots),
        grid=(pieces * per,),
        in_specs=[pl.BlockSpec(memory_space=pltpu.SMEM)]
        + in_vmem(len(ins))
        + [pl.BlockSpec((width, chunk), lambda i, p=p: (0, at(p, i))) for p in range(pieces)]
        + [pl.BlockSpec((chunk, width), lambda i, p=p: (at(p, i), 0)) for p in range(pieces)],
        out_specs=in_vmem(len(ins)),
        out_shape=[jax.ShapeDtypeStruct(a.shape, jnp.bfloat16) for a in ins],
        scratch_shapes=[
            pltpu.VMEM((rows, width), jnp.bfloat16),
            pltpu.VMEM((rows, width), jnp.float32),
        ],
        compiler_params=pltpu.CompilerParams(
            dimension_semantics=("arbitrary",), vmem_limit_bytes=VMEM_LIMIT
        ),
        cost_estimate=cost(2 * rows * width * hidden * pieces, *first, *second),
    )(live, *ins, *first, *second)


def body(
    tokens,
    lengths,
    target,
    lang_group,
    blocks,
    enc_gain,
    w_query,
    w_key,
    w_value,
    w_output,
    moe_gain,
    expert_in,
    expert_out,
):
    count, width = tokens.shape
    lang_count, fsdp_count = lax.axis_size("lang"), lax.axis_size("fsdp")
    lang_at, fsdp_at = lax.axis_index("lang"), lax.axis_index("fsdp")
    slots_dev = min(32, lang_count // 2)
    capacity = count // slots_dev
    direct = lang_count <= 16 and lang_count & (lang_count - 1) == 0 and capacity % 16 == 0
    fsdp_scalar = fsdp_at.astype(jnp.int32).reshape(1)
    lang_scalar = lang_at.astype(jnp.int32).reshape(1)

    def others(shard):
        return [
            lax.ppermute(shard, "fsdp", [(i, (i + s) % fsdp_count) for i in range(fsdp_count)])
            for s in range(1, fsdp_count)
        ]

    ends = jnp.cumsum(lengths)
    positions = jnp.arange(count, dtype=jnp.int32)
    sentence = jnp.sum((positions[:, None] >= ends[None, :]).astype(jnp.int32), axis=1)
    lang_ids = jnp.arange(lang_group.shape[0], dtype=jnp.int32)
    sent_group = jnp.sum(
        jnp.where(target[:, None] == lang_ids[None, :], lang_group[None, :], 0), axis=1
    )
    run_ids = jnp.arange(slots_dev, dtype=jnp.int32)
    run_sent = jnp.sum((run_ids[:, None] * capacity >= ends[None, :]).astype(jnp.int32), axis=1)
    sent_ids = jnp.arange(lengths.shape[0], dtype=jnp.int32)
    run_group = jnp.sum(
        jnp.where(run_sent[:, None] == sent_ids[None, :], sent_group[None, :], 0), axis=1
    )
    group_ids = jnp.arange(lang_count, dtype=jnp.int32)
    half = lang_count // 2
    slot_group = jnp.where(
        group_ids < half,
        lang_at // half * half + group_ids,
        jnp.bitwise_xor(group_ids, lang_at.astype(jnp.int32)),
    )
    run_of_slot = slots_dev - jnp.sum(
        jnp.where(run_group[None, :] == slot_group[:, None], slots_dev - run_ids[None, :], 0),
        axis=1,
    )
    weights = (w_query, w_key, w_value)
    later = [others(w) for w in weights]
    output_w = [w_output, *others(w_output)]
    rest, sums = project(fsdp_scalar, tokens, enc_gain[None, :], weights, fsdp_count)
    block = 128 if count % 128 == 0 and 128 % capacity == 0 else count
    keys = sentence.reshape(count // block, 1, block)
    same = sentence.reshape(count // block, block, 1) == keys
    bias = jnp.where(same, jnp.float32(0), jnp.float32(-1e30)).reshape(count, block)
    bias, run_of_slot, later = lax.optimization_barrier((bias, run_of_slot, later))
    context = attend(bias, rest, sums, later)
    context, output_w, *shards = lax.optimization_barrier(
        (context, output_w, expert_in[0], expert_out[0])
    )
    first, second = ([shard, *others(shard)] for shard in shards)
    hidden, slots = hidden_states(
        fsdp_scalar, run_of_slot, context, tokens, moe_gain[None, :], output_w, slots_dev,
        lang_count if direct else 0,
    )

    def swap(ks, arrays):
        return [
            lax.ppermute(a, "lang", [(i, i ^ k) for i in range(lang_count)])
            for k, a in zip(ks, arrays)
        ]

    if direct:

        def within(array):
            halves = [list(range(top, top + half)) for top in (0, half)]
            return lax.all_to_all(
                array, "lang", 0, 0, axis_index_groups=halves, tiled=True
            )

        def after(arrays, *done):
            return list(lax.optimization_barrier((tuple(arrays), done))[0])

        quarter = half // 2
        far, last = range(half, half + quarter), range(half + quarter, lang_count)
        near_in = within(slots[0])
        far_in = swap(far, slots[1 : 1 + quarter])
        last_in = swap(last, after(slots[1 + quarter :], *far_in[:3]))
        far_out = expert_ffn(far_in, first, second)
        far_out, live = live_rows(lang_scalar, blocks, near_in, [*far_in, *last_in], far_out)
        ins = after([near_in.reshape(half * capacity, width), *last_in], far_out)
        far_back = swap(far, far_out)
        held = [list(range(half)), *[[k] for k in last]]
        near_out, *last_out = expert_ffn(ins, first, second, live, held)
        near_out, *last_out = after([near_out, *last_out], far_back)
        last_back = swap(last, last_out)
        near_back = within(near_out.reshape(half, capacity, width))
        return mix(run_of_slot, hidden, near_back, far_back + last_back, slots_dev)

    dispatch = (group_ids[:, None] == run_group[None, :]).astype(jnp.bfloat16)
    runs = slots[0].reshape(slots_dev, capacity * width)
    outgoing = jnp.dot(dispatch, runs, preferred_element_type=jnp.float32).astype(jnp.bfloat16)
    used = jnp.any(dispatch > 0, axis=1, keepdims=True)
    outgoing = jnp.where(used, outgoing, jnp.bfloat16(EMPTY))
    incoming = lax.all_to_all(
        outgoing.reshape(lang_count, capacity, width), "lang", 0, 0, tiled=True
    )
    full = (incoming[:, 0, 0] < EMPTY / 2).astype(jnp.int32)
    live = (jnp.cumsum(full) - full) * capacity // BLOCK < blocks[0, 0]
    (result,) = expert_ffn([incoming.reshape(lang_count * capacity, width)], first, second)
    result = jnp.where(live[:, None, None], result.reshape(lang_count, capacity, width), 0)
    back = lax.all_to_all(result.astype(jnp.bfloat16), "lang", 0, 0, tiled=True)
    expert = lax.dot_general(
        dispatch,
        back.reshape(lang_count, capacity * width),
        (((0,), (0,)), ((), ())),
        preferred_element_type=jnp.float32,
    ).reshape(count, width)
    return (hidden.astype(jnp.float32) + expert).astype(jnp.bfloat16)


def solution(mesh):
    return jax.shard_map(
        body,
        mesh=mesh,
        in_specs=(
            P(("lang", "fsdp"), None),
            P(("lang", "fsdp")),
            P(("lang", "fsdp")),
            P(),
            P("lang", "fsdp"),
            P(),
            P("fsdp", None),
            P("fsdp", None),
            P("fsdp", None),
            P("fsdp", None),
            P(),
            P("lang", None, "fsdp"),
            P("lang", "fsdp", None),
        ),
        out_specs=P(("lang", "fsdp"), None),
        check_vma=False,
    )
```

```python
import functools

import jax
import jax.numpy as jnp
from jax import lax
from jax.experimental import pallas as pl
from jax.experimental.pallas import tpu as pltpu
from jax.sharding import PartitionSpec as P

HDIM = 128
BLOCK = 128
VMEM_LIMIT = 42 * 1024 * 1024
FRONT_LIMIT = 24 * 1024 * 1024

EMPTY = 1024.0

epsilon = 1e-05


def layer_norm(values, gain):
    floats = values.astype(jnp.float32)
    center = floats - jnp.mean(floats, axis=-1, keepdims=True)
    spread = jnp.mean(center * center, axis=-1, keepdims=True)
    return center * lax.rsqrt(spread + epsilon) * gain


def dot(a, b):
    return jnp.dot(a, b, preferred_element_type=jnp.float32)


def in_vmem(count):
    return [pl.BlockSpec(memory_space=pltpu.VMEM)] * count


def cost(macs, *arrays):
    size = sum(a.size * a.dtype.itemsize for a in arrays)
    return pl.CostEstimate(flops=2 * macs, bytes_accessed=size, transcendentals=0)


def project_kernel(pieces, at_ref, tokens, gain, *refs):
    weights, rest, sums = refs[:3], refs[3 : 2 + pieces], refs[2 + pieces : 5 + pieces]
    own = refs[-1]
    part = own.shape[1]
    normed = layer_norm(tokens[...], gain[...]).astype(jnp.bfloat16)
    for v in range(pieces):

        @pl.when(at_ref[0] == v)
        def _():
            for s, ref in enumerate((own, *rest)):
                first = (v - s) % pieces * part
                ref[...] = normed[:, first : first + part]

    for weight, total in zip(weights, sums):
        total[...] = dot(own[...], weight[...])


def project(at, tokens, gain, weights, pieces):
    count, width = tokens.shape
    part, wide = weights[0].shape
    out = pl.pallas_call(
        functools.partial(project_kernel, pieces),
        in_specs=[pl.BlockSpec(memory_space=pltpu.SMEM)]
        + in_vmem(5),
        out_specs=in_vmem(pieces + 2),
        out_shape=[jax.ShapeDtypeStruct((count, part), jnp.bfloat16)] * (pieces - 1)
        + [jax.ShapeDtypeStruct((count, wide), jnp.float32)] * 3,
        scratch_shapes=[pltpu.VMEM((count, part), jnp.bfloat16)],
        compiler_params=pltpu.CompilerParams(vmem_limit_bytes=FRONT_LIMIT),
        cost_estimate=cost(3 * count * part * wide, tokens, *weights),
    )(at, tokens, gain, *weights)
    return out[: pieces - 1], out[pieces - 1 :]


def attend_kernel(rest_count, bias, *refs):
    rest = refs[:rest_count]
    sums = refs[rest_count : rest_count + 3]
    weights = refs[rest_count + 3 : -2]
    context, scores = refs[-2:]

    def full(n):
        total = sums[n][...]
        for s in range(rest_count):
            total += dot(rest[s][...], weights[n * rest_count + s][...])
        return total.astype(jnp.bfloat16)

    count, block = bias.shape
    query, keyed = full(0), full(1)
    heads = query.shape[1] // HDIM
    tiles = [
        (h, slice(h * HDIM, (h + 1) * HDIM), slice(top, top + block))
        for h in range(heads)
        for top in range(0, count, block)
    ]
    for h, head, rows in tiles:
        product = lax.dot_general(
            query[rows, head], keyed[rows, head], (((1,), (1,)), ((), ())),
            preferred_element_type=jnp.float32,
        )
        scores[h, rows, :] = product * (HDIM**-0.5) + bias[rows, :]
    valued = full(2)
    for h, head, rows in tiles:
        tile = scores[h, rows, :]
        weight = jnp.exp(tile - jnp.max(tile, axis=-1, keepdims=True))
        probs = (weight / jnp.sum(weight, axis=-1, keepdims=True)).astype(jnp.bfloat16)
        context[rows, head] = dot(probs, valued[rows, head]).astype(jnp.bfloat16)


def attend(bias, rest, sums, weights):
    count, wide = sums[0].shape
    flat = [w for pieces in weights for w in pieces]
    return pl.pallas_call(
        functools.partial(attend_kernel, len(rest)),
        in_specs=in_vmem(4 + len(rest) + len(flat)),
        out_specs=in_vmem(1)[0],
        out_shape=jax.ShapeDtypeStruct((count, wide), jnp.bfloat16),
        scratch_shapes=[pltpu.VMEM((wide // HDIM, *bias.shape), jnp.float32)],
        compiler_params=pltpu.CompilerParams(vmem_limit_bytes=FRONT_LIMIT),
        cost_estimate=cost(2 * count * sum(w.size for w in flat), *flat, *sums),
    )(bias, *rest, *sums, *flat)


def hidden_kernel(pieces, runs, slots, at_ref, run_ref, context, tokens, gain, *refs):
    weights, hidden, outs, routed = refs[:pieces], refs[pieces], refs[pieces + 1 : -1], refs[-1]
    part = weights[0].shape[0]
    count = tokens.shape[0]
    total = tokens[...].astype(jnp.float32)
    for s in range(pieces):
        first = lax.rem(at_ref[0] + pieces - s, pieces) * part
        total += dot(context[:, pl.ds(pl.multiple_of(first, 128), part)], weights[s][...])
    hidden[...] = total.astype(jnp.bfloat16)
    rows = count // runs
    for j in range(runs):
        run = slice(j * rows, (j + 1) * rows)
        normed = layer_norm(hidden[run, :], gain[...]).astype(jnp.bfloat16)
        if slots:
            routed[j] = normed
        else:
            outs[0][run, :] = normed
    if slots:
        routed[runs] = jnp.full_like(routed[runs], EMPTY)
        near = outs[0].shape[0]
        for k in range(slots):
            if k < near:
                outs[0][k] = routed[run_ref[k]]
            else:
                outs[1 + k - near][...] = routed[run_ref[k]]


def hidden_states(at, run_of_slot, context, tokens, gain, weights, runs, slots):
    count, width = tokens.shape
    rows = count // runs
    near = slots // 2
    outs = [(near, rows, width)] + [(rows, width)] * near if slots else [(count, width)]
    out = pl.pallas_call(
        functools.partial(hidden_kernel, len(weights), runs, slots),
        in_specs=[pl.BlockSpec(memory_space=pltpu.SMEM)] * 2 + in_vmem(3 + len(weights)),
        out_specs=in_vmem(1 + len(outs)),
        out_shape=[
            jax.ShapeDtypeStruct(shape, jnp.bfloat16) for shape in [tokens.shape, *outs]
        ],
        scratch_shapes=[pltpu.VMEM((runs + 1, rows, width), jnp.bfloat16)],
        compiler_params=pltpu.CompilerParams(vmem_limit_bytes=FRONT_LIMIT),
        cost_estimate=cost(context.size * width, context, tokens, *weights),
    )(at, run_of_slot, context, tokens, gain, *weights)
    return out[0], out[1:]


def mix_kernel(runs, run_ref, hidden, near, *refs):
    far, mixed = refs[:-1], refs[-1]
    rows = hidden.shape[0] // runs
    half = near.shape[0]
    for k in range(half + len(far)):

        @pl.when(run_ref[k] < runs)
        def _():
            run = pl.ds(pl.multiple_of(run_ref[k] * rows, rows), rows)
            expert = near[k] if k < half else far[k - half][...]
            total = hidden[run, :].astype(jnp.float32) + expert.astype(jnp.float32)
            mixed[run, :] = total.astype(jnp.bfloat16)


def mix(run_of_slot, hidden, near, far, runs):
    return pl.pallas_call(
        functools.partial(mix_kernel, runs),
        in_specs=[pl.BlockSpec(memory_space=pltpu.SMEM)] + in_vmem(2 + len(far)),
        out_specs=in_vmem(1)[0],
        out_shape=jax.ShapeDtypeStruct(hidden.shape, jnp.bfloat16),
        compiler_params=pltpu.CompilerParams(vmem_limit_bytes=FRONT_LIMIT),
    )(run_of_slot, hidden, near, *far)


def live_kernel(first, at_ref, blocks_ref, near, *refs):
    count = len(refs) - 1 - 2 * first
    far, results, outs, live = refs[:count], refs[count : count + first], refs[-1 - first : -1], refs[-1]
    half, rows = near.shape[:2]
    me = at_ref[0]
    heads = [near[k, :16, :128] for k in range(half)] + [ref[:16, :128] for ref in far]
    full = [(jnp.max(head.astype(jnp.float32)) < EMPTY / 2).astype(jnp.int32) for head in heads]
    source = [me // half * half + k for k in range(half)]
    source += [jnp.bitwise_xor(me, half + k) for k in range(len(far))]
    for k in range(half + len(far)):
        before = sum(jnp.where(s < source[k], f, 0) for s, f in zip(source, full))
        live[k] = (before * rows // BLOCK < blocks_ref[0, 0]).astype(jnp.int32)
    for k in range(half):
        part = slice(k * rows, (k + 1) * rows)
        kept = live[k] > 0
        outs[0][k] = jnp.where(kept, results[0][part, :], jnp.zeros_like(outs[0][k]))
    for k in range(1, first):
        kept = live[half + k - 1] > 0
        outs[k][...] = jnp.where(kept, results[k][...], jnp.zeros_like(results[k]))


def live_rows(at, blocks, near, far, results):
    first = len(results)
    smem = pl.BlockSpec(memory_space=pltpu.SMEM)
    out = pl.pallas_call(
        functools.partial(live_kernel, first),
        in_specs=[smem] * 2 + in_vmem(1 + len(far) + first),
        out_specs=in_vmem(first) + [smem],
        out_shape=[jax.ShapeDtypeStruct(r.shape, r.dtype) for r in (near, *results[1:])]
        + [jax.ShapeDtypeStruct((near.shape[0] + len(far),), jnp.int32)],
        compiler_params=pltpu.CompilerParams(vmem_limit_bytes=FRONT_LIMIT),
    )(at, blocks, near, *far, *results)
    return out[:first], out[first]


def expert_kernel(sizes, pieces, per, slots, live, *refs):
    count = len(sizes)
    ins, outs = refs[:count], refs[count + 2 * pieces : 2 * count + 2 * pieces]
    first, second = refs[count : count + pieces], refs[count + pieces : count + 2 * pieces]
    packed, total = refs[-2:]
    step = pl.program_id(0)
    tops = [sum(sizes[:n]) for n in range(count)]

    @pl.when(step == 0)
    def _():
        for top, size, ref in zip(tops, sizes, ins):
            packed[top : top + size, :] = ref[...]
        total[...] = jnp.zeros_like(total)

    for p in range(pieces):

        @pl.when(step // per == p)
        def _():
            inner = jnp.maximum(dot(packed[...], first[p][...]), 0.0).astype(jnp.bfloat16)
            total[...] += dot(inner, second[p][...])

    @pl.when(step == pieces * per - 1)
    def _():
        for n, (top, size, ref) in enumerate(zip(tops, sizes, outs)):
            rows = size // max(1, len(slots[n]))
            for m, slot in enumerate(slots[n]):
                part = slice(top + m * rows, top + (m + 1) * rows)
                kept = jnp.where(live[slot] > 0, total[part, :], 0.0)
                ref[m * rows : (m + 1) * rows, :] = kept.astype(jnp.bfloat16)
            if not slots[n]:
                ref[...] = total[top : top + size, :].astype(jnp.bfloat16)


def expert_ffn(ins, first, second, live=None, slots=None):
    pieces, (width, hidden) = len(first), first[0].shape
    sizes = [a.shape[0] for a in ins]
    rows = sum(sizes)
    chunk = 1024 if rows <= 256 else 512
    chunk = chunk if hidden % chunk == 0 else hidden
    per = hidden // chunk
    if live is None:
        live, slots = jnp.zeros((1,), jnp.int32), [[]] * len(ins)

    def at(p, i):
        return jnp.clip(i - p * per, 0, per - 1)

    return pl.pallas_call(
        functools.partial(expert_kernel, sizes, pieces, per, slots),
        grid=(pieces * per,),
        in_specs=[pl.BlockSpec(memory_space=pltpu.SMEM)]
        + in_vmem(len(ins))
        + [pl.BlockSpec((width, chunk), lambda i, p=p: (0, at(p, i))) for p in range(pieces)]
        + [pl.BlockSpec((chunk, width), lambda i, p=p: (at(p, i), 0)) for p in range(pieces)],
        out_specs=in_vmem(len(ins)),
        out_shape=[jax.ShapeDtypeStruct(a.shape, jnp.bfloat16) for a in ins],
        scratch_shapes=[
            pltpu.VMEM((rows, width), jnp.bfloat16),
            pltpu.VMEM((rows, width), jnp.float32),
        ],
        compiler_params=pltpu.CompilerParams(
            dimension_semantics=("arbitrary",), vmem_limit_bytes=VMEM_LIMIT
        ),
        cost_estimate=cost(2 * rows * width * hidden * pieces, *first, *second),
    )(live, *ins, *first, *second)


def body(
    tokens,
    lengths,
    target,
    lang_group,
    blocks,
    enc_gain,
    w_query,
    w_key,
    w_value,
    w_output,
    moe_gain,
    expert_in,
    expert_out,
):
    count, width = tokens.shape
    lang_count, fsdp_count = lax.axis_size("lang"), lax.axis_size("fsdp")
    lang_at, fsdp_at = lax.axis_index("lang"), lax.axis_index("fsdp")
    slots_dev = min(32, lang_count // 2)
    capacity = count // slots_dev
    direct = lang_count <= 16 and lang_count & (lang_count - 1) == 0 and capacity % 16 == 0
    fsdp_scalar = fsdp_at.astype(jnp.int32).reshape(1)
    lang_scalar = lang_at.astype(jnp.int32).reshape(1)

    def others(shard):
        return [
            lax.ppermute(shard, "fsdp", [(i, (i + s) % fsdp_count) for i in range(fsdp_count)])
            for s in range(1, fsdp_count)
        ]

    ends = jnp.cumsum(lengths)
    positions = jnp.arange(count, dtype=jnp.int32)
    sentence = jnp.sum((positions[:, None] >= ends[None, :]).astype(jnp.int32), axis=1)
    lang_ids = jnp.arange(lang_group.shape[0], dtype=jnp.int32)
    sent_group = jnp.sum(
        jnp.where(target[:, None] == lang_ids[None, :], lang_group[None, :], 0), axis=1
    )
    run_ids = jnp.arange(slots_dev, dtype=jnp.int32)
    run_sent = jnp.sum((run_ids[:, None] * capacity >= ends[None, :]).astype(jnp.int32), axis=1)
    sent_ids = jnp.arange(lengths.shape[0], dtype=jnp.int32)
    run_group = jnp.sum(
        jnp.where(run_sent[:, None] == sent_ids[None, :], sent_group[None, :], 0), axis=1
    )
    group_ids = jnp.arange(lang_count, dtype=jnp.int32)
    half = lang_count // 2
    slot_group = jnp.where(
        group_ids < half,
        lang_at // half * half + group_ids,
        jnp.bitwise_xor(group_ids, lang_at.astype(jnp.int32)),
    )
    run_of_slot = slots_dev - jnp.sum(
        jnp.where(run_group[None, :] == slot_group[:, None], slots_dev - run_ids[None, :], 0),
        axis=1,
    )
    weights = (w_query, w_key, w_value)
    later = [others(w) for w in weights]
    output_w = [w_output, *others(w_output)]
    rest, sums = project(fsdp_scalar, tokens, enc_gain[None, :], weights, fsdp_count)
    block = 128 if count % 128 == 0 and 128 % capacity == 0 else count
    keys = sentence.reshape(count // block, 1, block)
    same = sentence.reshape(count // block, block, 1) == keys
    bias = jnp.where(same, jnp.float32(0), jnp.float32(-1e30)).reshape(count, block)
    bias, run_of_slot, later = lax.optimization_barrier((bias, run_of_slot, later))
    context = attend(bias, rest, sums, later)
    context, output_w, *shards = lax.optimization_barrier(
        (context, output_w, expert_in[0], expert_out[0])
    )
    first, second = ([shard, *others(shard)] for shard in shards)
    hidden, slots = hidden_states(
        fsdp_scalar, run_of_slot, context, tokens, moe_gain[None, :], output_w, slots_dev,
        lang_count if direct else 0,
    )

    def swap(ks, arrays):
        return [
            lax.ppermute(a, "lang", [(i, i ^ k) for i in range(lang_count)])
            for k, a in zip(ks, arrays)
        ]

    if direct:

        def within(array):
            halves = [list(range(top, top + half)) for top in (0, half)]
            return lax.all_to_all(
                array, "lang", 0, 0, axis_index_groups=halves, tiled=True
            )

        def after(arrays, *done):
            return list(lax.optimization_barrier((tuple(arrays), done))[0])

        quarter = half * 3 // 8
        far, last = range(half, half + quarter), range(half + quarter, lang_count)
        far_in = swap(far, slots[1 : 1 + quarter])
        near_in = within(slots[0])
        last_in = []
        for n, k in enumerate(last):
            done = far_in[min(n, quarter - 1)]
            last_in += swap([k], after([slots[1 + quarter + n]], done))
        ins = [near_in.reshape(half * capacity, width), *far_in]
        out = expert_ffn(ins, first, second)
        (near_out, *far_out), live = live_rows(lang_scalar, blocks, near_in, [*far_in, *last_in], out)
        last_in = after(last_in, far_out)
        far_back = swap(far, far_out)
        near_back = within(near_out)
        last_out = expert_ffn(last_in, first, second, live, [[k] for k in last])
        last_back = swap(last, after(last_out, far_back))
        return mix(run_of_slot, hidden, near_back, far_back + last_back, slots_dev)

    dispatch = (group_ids[:, None] == run_group[None, :]).astype(jnp.bfloat16)
    runs = slots[0].reshape(slots_dev, capacity * width)
    outgoing = jnp.dot(dispatch, runs, preferred_element_type=jnp.float32).astype(jnp.bfloat16)
    used = jnp.any(dispatch > 0, axis=1, keepdims=True)
    outgoing = jnp.where(used, outgoing, jnp.bfloat16(EMPTY))
    incoming = lax.all_to_all(
        outgoing.reshape(lang_count, capacity, width), "lang", 0, 0, tiled=True
    )
    full = (incoming[:, 0, 0] < EMPTY / 2).astype(jnp.int32)
    live = (jnp.cumsum(full) - full) * capacity // BLOCK < blocks[0, 0]
    (result,) = expert_ffn([incoming.reshape(lang_count * capacity, width)], first, second)
    result = jnp.where(live[:, None, None], result.reshape(lang_count, capacity, width), 0)
    back = lax.all_to_all(result.astype(jnp.bfloat16), "lang", 0, 0, tiled=True)
    expert = lax.dot_general(
        dispatch,
        back.reshape(lang_count, capacity * width),
        (((0,), (0,)), ((), ())),
        preferred_element_type=jnp.float32,
    ).reshape(count, width)
    return (hidden.astype(jnp.float32) + expert).astype(jnp.bfloat16)


def solution(mesh):
    return jax.shard_map(
        body,
        mesh=mesh,
        in_specs=(
            P(("lang", "fsdp"), None),
            P(("lang", "fsdp")),
            P(("lang", "fsdp")),
            P(),
            P("lang", "fsdp"),
            P(),
            P("fsdp", None),
            P("fsdp", None),
            P("fsdp", None),
            P("fsdp", None),
            P(),
            P("lang", None, "fsdp"),
            P("lang", "fsdp", None),
        ),
        out_specs=P(("lang", "fsdp"), None),
        check_vma=False,
    )
```

```python
import functools

import jax
import jax.numpy as jnp
from jax import lax
from jax.experimental import pallas as pl
from jax.experimental.pallas import tpu as pltpu
from jax.sharding import PartitionSpec as P

HDIM = 128
BLOCK = 128
VMEM_LIMIT = 42 * 1024 * 1024
FRONT_LIMIT = 24 * 1024 * 1024

EMPTY = 1024.0

epsilon = 1e-05


def layer_norm(values, gain):
    floats = values.astype(jnp.float32)
    center = floats - jnp.mean(floats, axis=-1, keepdims=True)
    spread = jnp.mean(center * center, axis=-1, keepdims=True)
    return center * lax.rsqrt(spread + epsilon) * gain


def dot(a, b):
    return jnp.dot(a, b, preferred_element_type=jnp.float32)


def in_vmem(count):
    return [pl.BlockSpec(memory_space=pltpu.VMEM)] * count


def hbm(array):
    return pltpu.with_memory_space_constraint(array, pltpu.HBM)


def vmem(array):
    return pltpu.with_memory_space_constraint(array, pltpu.VMEM)


def in_hbm(count):
    return [pl.BlockSpec(memory_space=pltpu.HBM)] * count


def fetch(refs, held, arrived):
    copies = [
        pltpu.make_async_copy(ref, held.at[n], arrived.at[n]) for n, ref in enumerate(refs)
    ]
    for copy in copies:
        copy.start()
    return copies


def cost(macs, *arrays):
    size = sum(a.size * a.dtype.itemsize for a in arrays)
    return pl.CostEstimate(flops=2 * macs, bytes_accessed=size, transcendentals=0)


def project_kernel(pieces, at_ref, tokens, gain, *refs):
    weights, rest, sums = refs[:3], refs[3 : 2 + pieces], refs[2 + pieces : 5 + pieces]
    own, held, arrived = refs[-3:]
    part = own.shape[1]
    copies = fetch(weights, held, arrived)
    normed = layer_norm(tokens[...], gain[...]).astype(jnp.bfloat16)
    for v in range(pieces):

        @pl.when(at_ref[0] == v)
        def _():
            for s, ref in enumerate((own, *rest)):
                first = (v - s) % pieces * part
                ref[...] = normed[:, first : first + part]

    for n, total in enumerate(sums):
        copies[n].wait()
        total[...] = dot(own[...], held[n])


def project(at, tokens, gain, weights, pieces):
    count, width = tokens.shape
    part, wide = weights[0].shape
    out = pl.pallas_call(
        functools.partial(project_kernel, pieces),
        in_specs=[pl.BlockSpec(memory_space=pltpu.SMEM)] + in_vmem(2) + in_hbm(3),
        out_specs=in_vmem(pieces + 2),
        out_shape=[pltpu.VMEM((count, part), jnp.bfloat16)] * (pieces - 1)
        + [pltpu.VMEM((count, wide), jnp.float32)] * 3,
        scratch_shapes=[
            pltpu.VMEM((count, part), jnp.bfloat16),
            pltpu.VMEM((3, part, wide), jnp.bfloat16),
            pltpu.SemaphoreType.DMA((3,)),
        ],
        compiler_params=pltpu.CompilerParams(vmem_limit_bytes=FRONT_LIMIT),
        cost_estimate=cost(3 * count * part * wide, tokens, *weights),
    )(at, tokens, gain, *map(hbm, weights))
    return out[: pieces - 1], out[pieces - 1 :]


def attend_kernel(rest_count, bias, *refs):
    rest = refs[:rest_count]
    sums = refs[rest_count : rest_count + 3]
    weights = refs[rest_count + 3 : -4]
    context, scores, held, arrived = refs[-4:]
    copies = fetch(weights, held, arrived)

    def full(n):
        total = sums[n][...]
        for s in range(rest_count):
            copies[n * rest_count + s].wait()
            total += dot(rest[s][...], held[n * rest_count + s])
        return total.astype(jnp.bfloat16)

    count, block = bias.shape
    query, keyed = full(0), full(1)
    heads = query.shape[1] // HDIM
    tiles = [
        (h, slice(h * HDIM, (h + 1) * HDIM), slice(top, top + block))
        for h in range(heads)
        for top in range(0, count, block)
    ]
    for h, head, rows in tiles:
        product = lax.dot_general(
            query[rows, head], keyed[rows, head], (((1,), (1,)), ((), ())),
            preferred_element_type=jnp.float32,
        )
        scores[h, rows, :] = product * (HDIM**-0.5) + bias[rows, :]
    valued = full(2)
    for h, head, rows in tiles:
        tile = scores[h, rows, :]
        weight = jnp.exp(tile - jnp.max(tile, axis=-1, keepdims=True))
        probs = (weight * (1.0 / jnp.sum(weight, axis=-1, keepdims=True))).astype(jnp.bfloat16)
        context[rows, head] = dot(probs, valued[rows, head]).astype(jnp.bfloat16)


def attend(bias, rest, sums, weights):
    count, wide = sums[0].shape
    flat = [w for pieces in weights for w in pieces]
    return pl.pallas_call(
        functools.partial(attend_kernel, len(rest)),
        in_specs=in_vmem(4 + len(rest)) + in_hbm(len(flat)),
        out_specs=in_vmem(1)[0],
        out_shape=pltpu.VMEM((count, wide), jnp.bfloat16),
        scratch_shapes=[
            pltpu.VMEM((wide // HDIM, *bias.shape), jnp.float32),
            pltpu.VMEM((len(flat), *flat[0].shape), jnp.bfloat16),
            pltpu.SemaphoreType.DMA((len(flat),)),
        ],
        compiler_params=pltpu.CompilerParams(vmem_limit_bytes=FRONT_LIMIT),
        cost_estimate=cost(2 * count * sum(w.size for w in flat), *flat, *sums),
    )(bias, *map(vmem, (*rest, *sums)), *map(hbm, flat))


def hidden_kernel(pieces, runs, slots, at_ref, run_ref, context, tokens, gain, *refs):
    weights, hidden, outs = refs[:pieces], refs[pieces], refs[pieces + 1 : -3]
    routed, held, arrived = refs[-3:]
    copies = fetch(weights, held, arrived)
    part = weights[0].shape[0]
    count = tokens.shape[0]
    total = tokens[...].astype(jnp.float32)
    for s in range(pieces):
        first = lax.rem(at_ref[0] + pieces - s, pieces) * part
        copies[s].wait()
        total += dot(context[:, pl.ds(pl.multiple_of(first, 128), part)], held[s])
    hidden[...] = total.astype(jnp.bfloat16)
    rows = count // runs
    for j in range(runs):
        run = slice(j * rows, (j + 1) * rows)
        normed = layer_norm(hidden[run, :], gain[...]).astype(jnp.bfloat16)
        if slots:
            routed[j] = normed
        else:
            outs[0][run, :] = normed
    if slots:
        routed[runs] = jnp.full_like(routed[runs], EMPTY)
        near = outs[0].shape[0]
        for k in range(slots):
            if k < near:
                outs[0][k] = routed[run_ref[k]]
            else:
                outs[1 + k - near][...] = routed[run_ref[k]]


def hidden_states(at, run_of_slot, context, tokens, gain, weights, runs, slots):
    count, width = tokens.shape
    rows = count // runs
    part = weights[0].shape[0]
    near = slots // 2
    outs = [(near, rows, width)] + [(rows, width)] * near if slots else [(count, width)]
    out = pl.pallas_call(
        functools.partial(hidden_kernel, len(weights), runs, slots),
        in_specs=[pl.BlockSpec(memory_space=pltpu.SMEM)] * 2 + in_vmem(3) + in_hbm(len(weights)),
        out_specs=in_vmem(1 + len(outs)),
        out_shape=[
            jax.ShapeDtypeStruct(shape, jnp.bfloat16) for shape in [tokens.shape, *outs]
        ],
        scratch_shapes=[
            pltpu.VMEM((runs + 1, rows, width), jnp.bfloat16),
            pltpu.VMEM((len(weights), part, width), jnp.bfloat16),
            pltpu.SemaphoreType.DMA((len(weights),)),
        ],
        compiler_params=pltpu.CompilerParams(vmem_limit_bytes=FRONT_LIMIT),
        cost_estimate=cost(context.size * width, context, tokens, *weights),
    )(at, run_of_slot, vmem(context), tokens, gain, *map(hbm, weights))
    return out[0], out[1:]


def mix_kernel(runs, run_ref, hidden, near, *refs):
    far, mixed = refs[:-1], refs[-1]
    rows = hidden.shape[0] // runs
    half = near.shape[0]
    for k in range(half + len(far)):

        @pl.when(run_ref[k] < runs)
        def _():
            run = pl.ds(pl.multiple_of(run_ref[k] * rows, rows), rows)
            expert = near[k] if k < half else far[k - half][...]
            total = hidden[run, :].astype(jnp.float32) + expert.astype(jnp.float32)
            mixed[run, :] = total.astype(jnp.bfloat16)


def mix(run_of_slot, hidden, near, far, runs):
    return pl.pallas_call(
        functools.partial(mix_kernel, runs),
        in_specs=[pl.BlockSpec(memory_space=pltpu.SMEM)] + in_vmem(2 + len(far)),
        out_specs=in_vmem(1)[0],
        out_shape=jax.ShapeDtypeStruct(hidden.shape, jnp.bfloat16),
        compiler_params=pltpu.CompilerParams(vmem_limit_bytes=FRONT_LIMIT),
    )(run_of_slot, hidden, near, *far)


def live_kernel(first, at_ref, blocks_ref, near, *refs):
    count = len(refs) - 1 - 2 * first
    far, results, outs, live = refs[:count], refs[count : count + first], refs[-1 - first : -1], refs[-1]
    half, rows = near.shape[:2]
    me = at_ref[0]
    heads = [near[k, :16, :128] for k in range(half)] + [ref[:16, :128] for ref in far]
    full = [(jnp.max(head.astype(jnp.float32)) < EMPTY / 2).astype(jnp.int32) for head in heads]
    source = [me // half * half + k for k in range(half)]
    source += [jnp.bitwise_xor(me, half + k) for k in range(len(far))]
    for k in range(half + len(far)):
        before = sum(jnp.where(s < source[k], f, 0) for s, f in zip(source, full))
        live[k] = (before * rows // BLOCK < blocks_ref[0, 0]).astype(jnp.int32)
    for k in range(half):
        part = slice(k * rows, (k + 1) * rows)
        kept = live[k] > 0
        outs[0][k] = jnp.where(kept, results[0][part, :], jnp.zeros_like(outs[0][k]))
    for k in range(1, first):
        kept = live[half + k - 1] > 0
        outs[k][...] = jnp.where(kept, results[k][...], jnp.zeros_like(results[k]))


def live_rows(at, blocks, near, far, results):
    first = len(results)
    smem = pl.BlockSpec(memory_space=pltpu.SMEM)
    out = pl.pallas_call(
        functools.partial(live_kernel, first),
        in_specs=[smem] * 2 + in_vmem(1 + len(far) + first),
        out_specs=in_vmem(first) + [smem],
        out_shape=[jax.ShapeDtypeStruct(r.shape, r.dtype) for r in (near, *results[1:])]
        + [jax.ShapeDtypeStruct((near.shape[0] + len(far),), jnp.int32)],
        compiler_params=pltpu.CompilerParams(vmem_limit_bytes=FRONT_LIMIT),
    )(at, blocks, near, *far, *results)
    return out[:first], out[first]


def expert_kernel(sizes, pieces, per, slots, live, *refs):
    count = len(sizes)
    ins, outs = refs[:count], refs[count + 2 * pieces : 2 * count + 2 * pieces]
    first, second = refs[count : count + pieces], refs[count + pieces : count + 2 * pieces]
    packed, total = refs[-2:]
    step = pl.program_id(0)
    tops = [sum(sizes[:n]) for n in range(count)]

    @pl.when(step == 0)
    def _():
        for top, size, ref in zip(tops, sizes, ins):
            packed[top : top + size, :] = ref[...]
        total[...] = jnp.zeros_like(total)

    for p in range(pieces):

        @pl.when(step // per == p)
        def _():
            inner = jnp.maximum(dot(packed[...], first[p][...]), 0.0).astype(jnp.bfloat16)
            total[...] += dot(inner, second[p][...])

    @pl.when(step == pieces * per - 1)
    def _():
        for n, (top, size, ref) in enumerate(zip(tops, sizes, outs)):
            rows = size // max(1, len(slots[n]))
            for m, slot in enumerate(slots[n]):
                part = slice(top + m * rows, top + (m + 1) * rows)
                kept = jnp.where(live[slot] > 0, total[part, :], 0.0)
                ref[m * rows : (m + 1) * rows, :] = kept.astype(jnp.bfloat16)
            if not slots[n]:
                ref[...] = total[top : top + size, :].astype(jnp.bfloat16)


def expert_ffn(ins, first, second, live=None, slots=None):
    pieces, (width, hidden) = len(first), first[0].shape
    sizes = [a.shape[0] for a in ins]
    rows = sum(sizes)
    chunk = 1024 if rows <= 256 else 512
    chunk = chunk if hidden % chunk == 0 else hidden
    per = hidden // chunk
    if live is None:
        live, slots = jnp.zeros((1,), jnp.int32), [[]] * len(ins)

    def at(p, i):
        return jnp.clip(i - p * per, 0, per - 1)

    return pl.pallas_call(
        functools.partial(expert_kernel, sizes, pieces, per, slots),
        grid=(pieces * per,),
        in_specs=[pl.BlockSpec(memory_space=pltpu.SMEM)]
        + in_vmem(len(ins))
        + [pl.BlockSpec((width, chunk), lambda i, p=p: (0, at(p, i))) for p in range(pieces)]
        + [pl.BlockSpec((chunk, width), lambda i, p=p: (at(p, i), 0)) for p in range(pieces)],
        out_specs=in_vmem(len(ins)),
        out_shape=[jax.ShapeDtypeStruct(a.shape, jnp.bfloat16) for a in ins],
        scratch_shapes=[
            pltpu.VMEM((rows, width), jnp.bfloat16),
            pltpu.VMEM((rows, width), jnp.float32),
        ],
        compiler_params=pltpu.CompilerParams(
            dimension_semantics=("arbitrary",), vmem_limit_bytes=VMEM_LIMIT
        ),
        cost_estimate=cost(2 * rows * width * hidden * pieces, *first, *second),
    )(live, *ins, *map(hbm, first), *map(hbm, second))


def body(
    tokens,
    lengths,
    target,
    lang_group,
    blocks,
    enc_gain,
    w_query,
    w_key,
    w_value,
    w_output,
    moe_gain,
    expert_in,
    expert_out,
):
    count, width = tokens.shape
    lang_count, fsdp_count = lax.axis_size("lang"), lax.axis_size("fsdp")
    lang_at, fsdp_at = lax.axis_index("lang"), lax.axis_index("fsdp")
    slots_dev = min(32, lang_count // 2)
    capacity = count // slots_dev
    direct = lang_count <= 16 and lang_count & (lang_count - 1) == 0 and capacity % 16 == 0
    fsdp_scalar = fsdp_at.astype(jnp.int32).reshape(1)
    lang_scalar = lang_at.astype(jnp.int32).reshape(1)

    def others(shard):
        return [
            lax.ppermute(shard, "fsdp", [(i, (i + s) % fsdp_count) for i in range(fsdp_count)])
            for s in range(1, fsdp_count)
        ]

    ends = jnp.cumsum(lengths)
    positions = jnp.arange(count, dtype=jnp.int32)
    sentence = jnp.sum((positions[:, None] >= ends[None, :]).astype(jnp.int32), axis=1)
    lang_ids = jnp.arange(lang_group.shape[0], dtype=jnp.int32)
    sent_group = jnp.sum(
        jnp.where(target[:, None] == lang_ids[None, :], lang_group[None, :], 0), axis=1
    )
    run_ids = jnp.arange(slots_dev, dtype=jnp.int32)
    run_sent = jnp.sum((run_ids[:, None] * capacity >= ends[None, :]).astype(jnp.int32), axis=1)
    sent_ids = jnp.arange(lengths.shape[0], dtype=jnp.int32)
    run_group = jnp.sum(
        jnp.where(run_sent[:, None] == sent_ids[None, :], sent_group[None, :], 0), axis=1
    )
    group_ids = jnp.arange(lang_count, dtype=jnp.int32)
    half = lang_count // 2
    slot_group = jnp.where(
        group_ids < half,
        lang_at // half * half + group_ids,
        jnp.bitwise_xor(group_ids, lang_at.astype(jnp.int32)),
    )
    run_of_slot = slots_dev - jnp.sum(
        jnp.where(run_group[None, :] == slot_group[:, None], slots_dev - run_ids[None, :], 0),
        axis=1,
    )
    weights = (w_query, w_key, w_value)
    later = [others(w) for w in weights]
    output_w = [w_output, *others(w_output)]
    rest, sums = project(fsdp_scalar, tokens, enc_gain[None, :], weights, fsdp_count)
    block = 128 if count % 128 == 0 and 128 % capacity == 0 else count
    keys = sentence.reshape(count // block, 1, block)
    same = sentence.reshape(count // block, block, 1) == keys
    bias = jnp.where(same, jnp.float32(0), jnp.float32(-1e30)).reshape(count, block)
    bias, run_of_slot, later = lax.optimization_barrier((bias, run_of_slot, later))
    context = attend(bias, rest, sums, later)
    context, output_w, *shards = lax.optimization_barrier(
        (context, output_w, expert_in[0], expert_out[0])
    )
    first, second = ([shard, *others(shard)] for shard in shards)
    hidden, slots = hidden_states(
        fsdp_scalar, run_of_slot, context, tokens, moe_gain[None, :], output_w, slots_dev,
        lang_count if direct else 0,
    )

    def swap(ks, arrays):
        return [
            lax.ppermute(a, "lang", [(i, i ^ k) for i in range(lang_count)])
            for k, a in zip(ks, arrays)
        ]

    if direct:

        def within(array):
            halves = [list(range(top, top + half)) for top in (0, half)]
            return lax.all_to_all(
                array, "lang", 0, 0, axis_index_groups=halves, tiled=True
            )

        def after(arrays, *done):
            return list(lax.optimization_barrier((tuple(arrays), done))[0])

        quarter = half * 3 // 8
        far, last = range(half, half + quarter), range(half + quarter, lang_count)
        far_in = swap(far, slots[1 : 1 + quarter])
        near_in = within(slots[0])
        last_in = []
        for n, k in enumerate(last):
            done = far_in[min(n, quarter - 1)]
            last_in += swap([k], after([slots[1 + quarter + n]], done))
        ins = [near_in.reshape(half * capacity, width), *far_in]
        out = expert_ffn(ins, first, second)
        (near_out, *far_out), live = live_rows(lang_scalar, blocks, near_in, [*far_in, *last_in], out)
        last_in = after(last_in, far_out)
        far_back = swap(far, far_out)
        near_back = within(near_out)
        last_out = expert_ffn(last_in, first, second, live, [[k] for k in last])
        last_back = swap(last, after(last_out, far_back))
        return mix(run_of_slot, hidden, near_back, far_back + last_back, slots_dev)

    dispatch = (group_ids[:, None] == run_group[None, :]).astype(jnp.bfloat16)
    runs = slots[0].reshape(slots_dev, capacity * width)
    outgoing = jnp.dot(dispatch, runs, preferred_element_type=jnp.float32).astype(jnp.bfloat16)
    used = jnp.any(dispatch > 0, axis=1, keepdims=True)
    outgoing = jnp.where(used, outgoing, jnp.bfloat16(EMPTY))
    incoming = lax.all_to_all(
        outgoing.reshape(lang_count, capacity, width), "lang", 0, 0, tiled=True
    )
    full = (incoming[:, 0, 0] < EMPTY / 2).astype(jnp.int32)
    live = (jnp.cumsum(full) - full) * capacity // BLOCK < blocks[0, 0]
    (result,) = expert_ffn([incoming.reshape(lang_count * capacity, width)], first, second)
    result = jnp.where(live[:, None, None], result.reshape(lang_count, capacity, width), 0)
    back = lax.all_to_all(result.astype(jnp.bfloat16), "lang", 0, 0, tiled=True)
    expert = lax.dot_general(
        dispatch,
        back.reshape(lang_count, capacity * width),
        (((0,), (0,)), ((), ())),
        preferred_element_type=jnp.float32,
    ).reshape(count, width)
    return (hidden.astype(jnp.float32) + expert).astype(jnp.bfloat16)


def solution(mesh):
    return jax.shard_map(
        body,
        mesh=mesh,
        in_specs=(
            P(("lang", "fsdp"), None),
            P(("lang", "fsdp")),
            P(("lang", "fsdp")),
            P(),
            P("lang", "fsdp"),
            P(),
            P("fsdp", None),
            P("fsdp", None),
            P("fsdp", None),
            P("fsdp", None),
            P(),
            P("lang", None, "fsdp"),
            P("lang", "fsdp", None),
        ),
        out_specs=P(("lang", "fsdp"), None),
        check_vma=False,
    )
```

```python
import functools

import jax
import jax.numpy as jnp
from jax import lax
from jax.experimental import pallas as pl
from jax.experimental.pallas import tpu as pltpu
from jax.sharding import PartitionSpec as P

HDIM = 128
BLOCK = 128
AHEAD = 20_000_000_000
VMEM_LIMIT = 42 * 1024 * 1024
FRONT_LIMIT = 48 * 1024 * 1024

EMPTY = 1024.0

epsilon = 1e-05


def layer_norm(values, gain):
    floats = values.astype(jnp.float32)
    center = floats - jnp.mean(floats, axis=-1, keepdims=True)
    spread = jnp.mean(center * center, axis=-1, keepdims=True)
    return center * lax.rsqrt(spread + epsilon) * gain


def dot(a, b):
    return jnp.dot(a, b, preferred_element_type=jnp.float32)


def in_vmem(count):
    return [pl.BlockSpec(memory_space=pltpu.VMEM)] * count


def hbm(array):
    return pltpu.with_memory_space_constraint(array, pltpu.HBM)


def vmem(array):
    return pltpu.with_memory_space_constraint(array, pltpu.VMEM)


def in_hbm(count):
    return [pl.BlockSpec(memory_space=pltpu.HBM)] * count


def fetch(refs, held, arrived):
    copies = [
        pltpu.make_async_copy(ref, held.at[n], arrived.at[n]) for n, ref in enumerate(refs)
    ]
    for copy in copies:
        copy.start()
    return copies


def cost(macs, *arrays):
    size = sum(a.size * a.dtype.itemsize for a in arrays)
    return pl.CostEstimate(flops=2 * macs, bytes_accessed=size, transcendentals=0)


def project_kernel(pieces, at_ref, tokens, gain, *refs):
    weights, rest, sums = refs[:3], refs[3 : 2 + pieces], refs[2 + pieces : 5 + pieces]
    own, held, arrived = refs[-3:]
    part = own.shape[1]
    copies = fetch(weights, held, arrived)
    normed = layer_norm(tokens[...], gain[...]).astype(jnp.bfloat16)
    for v in range(pieces):

        @pl.when(at_ref[0] == v)
        def _():
            for s, ref in enumerate((own, *rest)):
                first = (v - s) % pieces * part
                ref[...] = normed[:, first : first + part]

    for n, total in enumerate(sums):
        copies[n].wait()
        total[...] = dot(own[...], held[n])


def project(at, tokens, gain, weights, pieces):
    count, width = tokens.shape
    part, wide = weights[0].shape
    out = pl.pallas_call(
        functools.partial(project_kernel, pieces),
        in_specs=[pl.BlockSpec(memory_space=pltpu.SMEM)] + in_vmem(2) + in_hbm(3),
        out_specs=in_vmem(pieces + 2),
        out_shape=[pltpu.VMEM((count, part), jnp.bfloat16)] * (pieces - 1)
        + [pltpu.VMEM((count, wide), jnp.float32)] * 3,
        scratch_shapes=[
            pltpu.VMEM((count, part), jnp.bfloat16),
            pltpu.VMEM((3, part, wide), jnp.bfloat16),
            pltpu.SemaphoreType.DMA((3,)),
        ],
        compiler_params=pltpu.CompilerParams(vmem_limit_bytes=FRONT_LIMIT),
        cost_estimate=cost(3 * count * part * wide, tokens, *weights),
    )(at, tokens, gain, *map(hbm, weights))
    return out[: pieces - 1], out[pieces - 1 :]


def attend_kernel(rest_count, bias, *refs):
    rest = refs[:rest_count]
    sums = refs[rest_count : rest_count + 3]
    weights = refs[rest_count + 3 : -4]
    context, scores, held, arrived = refs[-4:]
    copies = fetch(weights, held, arrived)

    def full(n):
        total = sums[n][...]
        for s in range(rest_count):
            copies[n * rest_count + s].wait()
            total += dot(rest[s][...], held[n * rest_count + s])
        return total.astype(jnp.bfloat16)

    count, block = bias.shape
    query, keyed = full(0), full(1)
    heads = query.shape[1] // HDIM
    tiles = [
        (h, slice(h * HDIM, (h + 1) * HDIM), slice(top, top + block))
        for h in range(heads)
        for top in range(0, count, block)
    ]
    for h, head, rows in tiles:
        product = lax.dot_general(
            query[rows, head], keyed[rows, head], (((1,), (1,)), ((), ())),
            preferred_element_type=jnp.float32,
        )
        scores[h, rows, :] = product * (HDIM**-0.5) + bias[rows, :]
    valued = full(2)
    for h, head, rows in tiles:
        tile = scores[h, rows, :]
        weight = jnp.exp(tile - jnp.max(tile, axis=-1, keepdims=True))
        probs = (weight * (1.0 / jnp.sum(weight, axis=-1, keepdims=True))).astype(jnp.bfloat16)
        context[rows, head] = dot(probs, valued[rows, head]).astype(jnp.bfloat16)


def attend(bias, rest, sums, weights):
    count, wide = sums[0].shape
    flat = [w for pieces in weights for w in pieces]
    return pl.pallas_call(
        functools.partial(attend_kernel, len(rest)),
        in_specs=in_vmem(4 + len(rest)) + in_hbm(len(flat)),
        out_specs=in_vmem(1)[0],
        out_shape=pltpu.VMEM((count, wide), jnp.bfloat16),
        scratch_shapes=[
            pltpu.VMEM((wide // HDIM, *bias.shape), jnp.float32),
            pltpu.VMEM((len(flat), *flat[0].shape), jnp.bfloat16),
            pltpu.SemaphoreType.DMA((len(flat),)),
        ],
        compiler_params=pltpu.CompilerParams(vmem_limit_bytes=FRONT_LIMIT),
        cost_estimate=cost(2 * count * sum(w.size for w in flat), *flat, *sums),
    )(bias, *map(vmem, (*rest, *sums)), *map(hbm, flat))


def hidden_kernel(pieces, runs, slots, at_ref, run_ref, context, tokens, gain, *refs):
    weights, hidden, outs = refs[:pieces], refs[pieces], refs[pieces + 1 : -3]
    routed, held, arrived = refs[-3:]
    copies = fetch(weights, held, arrived)
    part = weights[0].shape[0]
    count = tokens.shape[0]
    total = tokens[...].astype(jnp.float32)
    for s in range(pieces):
        first = lax.rem(at_ref[0] + pieces - s, pieces) * part
        copies[s].wait()
        total += dot(context[:, pl.ds(pl.multiple_of(first, 128), part)], held[s])
    hidden[...] = total.astype(jnp.bfloat16)
    rows = count // runs
    for j in range(runs):
        run = slice(j * rows, (j + 1) * rows)
        normed = layer_norm(hidden[run, :], gain[...]).astype(jnp.bfloat16)
        if slots:
            routed[j] = normed
        else:
            outs[0][run, :] = normed
    if slots:
        routed[runs] = jnp.full_like(routed[runs], EMPTY)
        near = outs[0].shape[0]
        for k in range(slots):
            if k < near:
                outs[0][k] = routed[run_ref[k]]
            else:
                outs[1 + k - near][...] = routed[run_ref[k]]


def hidden_states(at, run_of_slot, context, tokens, gain, weights, runs, slots):
    count, width = tokens.shape
    rows = count // runs
    part = weights[0].shape[0]
    near = slots // 2
    outs = [(near, rows, width)] + [(rows, width)] * near if slots else [(count, width)]
    out = pl.pallas_call(
        functools.partial(hidden_kernel, len(weights), runs, slots),
        in_specs=[pl.BlockSpec(memory_space=pltpu.SMEM)] * 2 + in_vmem(3) + in_hbm(len(weights)),
        out_specs=in_vmem(1 + len(outs)),
        out_shape=[
            jax.ShapeDtypeStruct(shape, jnp.bfloat16) for shape in [tokens.shape, *outs]
        ],
        scratch_shapes=[
            pltpu.VMEM((runs + 1, rows, width), jnp.bfloat16),
            pltpu.VMEM((len(weights), part, width), jnp.bfloat16),
            pltpu.SemaphoreType.DMA((len(weights),)),
        ],
        compiler_params=pltpu.CompilerParams(vmem_limit_bytes=FRONT_LIMIT),
        cost_estimate=cost(context.size * width, context, tokens, *weights),
    )(at, run_of_slot, vmem(context), tokens, gain, *map(hbm, weights))
    return out[0], out[1:]


def mix_kernel(runs, run_ref, base, *refs):
    ins, mixed = refs[:-1], refs[-1]
    rows = base.shape[0] // runs
    mixed[...] = base[...]
    for k, ref in enumerate(ins):

        @pl.when(run_ref[k] < runs)
        def _():
            run = pl.ds(pl.multiple_of(run_ref[k] * rows, rows), rows)
            total = base[run, :].astype(jnp.float32) + ref[...].astype(jnp.float32)
            mixed[run, :] = total.astype(jnp.bfloat16)


def near_mix_kernel(runs, run_ref, base, near, *refs):
    mix_kernel(runs, run_ref, base, *[near.at[k] for k in range(near.shape[0])], *refs)


def mix(run_of_slot, base, ins, runs, weight=0):
    kernel = near_mix_kernel if ins[0].ndim == 3 else mix_kernel
    return pl.pallas_call(
        functools.partial(kernel, runs),
        in_specs=[pl.BlockSpec(memory_space=pltpu.SMEM)] + in_vmem(1 + len(ins)),
        out_specs=in_vmem(1)[0],
        out_shape=jax.ShapeDtypeStruct(base.shape, jnp.bfloat16),
        compiler_params=pltpu.CompilerParams(vmem_limit_bytes=FRONT_LIMIT),
        cost_estimate=cost(weight, base, base, *ins),
    )(run_of_slot, base, *ins)


def stage_kernel(*refs):
    count = len(refs) // 2
    for ref, out in zip(refs[:count], refs[count:]):
        out[...] = ref[...]


def stage(arrays):
    return pl.pallas_call(
        stage_kernel,
        in_specs=in_vmem(len(arrays)),
        out_specs=in_vmem(len(arrays)),
        out_shape=[pltpu.VMEM(a.shape, a.dtype) for a in arrays],
        compiler_params=pltpu.CompilerParams(vmem_limit_bytes=FRONT_LIMIT),
        cost_estimate=cost(AHEAD, *arrays),
    )(*arrays)


def live_kernel(first, at_ref, blocks_ref, near, *refs):
    count = len(refs) - 1 - 2 * first
    far, results, outs, live = refs[:count], refs[count : count + first], refs[-1 - first : -1], refs[-1]
    half, rows = near.shape[:2]
    me = at_ref[0]
    heads = [near[k, :16, :128] for k in range(half)] + [ref[:16, :128] for ref in far]
    full = [(jnp.max(head.astype(jnp.float32)) < EMPTY / 2).astype(jnp.int32) for head in heads]
    source = [me // half * half + k for k in range(half)]
    source += [jnp.bitwise_xor(me, half + k) for k in range(len(far))]
    for k in range(half + len(far)):
        before = sum(jnp.where(s < source[k], f, 0) for s, f in zip(source, full))
        live[k] = (before * rows // BLOCK < blocks_ref[0, 0]).astype(jnp.int32)
    for k in range(first):
        kept = live[half + k] > 0
        outs[k][...] = jnp.where(kept, results[k][...], jnp.zeros_like(results[k]))


def live_rows(at, blocks, near, far, results):
    first = len(results)
    smem = pl.BlockSpec(memory_space=pltpu.SMEM)
    out = pl.pallas_call(
        functools.partial(live_kernel, first),
        in_specs=[smem] * 2 + in_vmem(1 + len(far) + first),
        out_specs=in_vmem(first) + [smem],
        out_shape=[jax.ShapeDtypeStruct(r.shape, r.dtype) for r in results]
        + [jax.ShapeDtypeStruct((near.shape[0] + len(far),), jnp.int32)],
        compiler_params=pltpu.CompilerParams(vmem_limit_bytes=FRONT_LIMIT),
    )(at, blocks, near, *far, *results)
    return out[:first], out[first]


def expert_kernel(sizes, pieces, per, slots, live, *refs):
    count = len(sizes)
    ins, outs = refs[:count], refs[count + 2 * pieces : 2 * count + 2 * pieces]
    first, second = refs[count : count + pieces], refs[count + pieces : count + 2 * pieces]
    packed, total = refs[-2:]
    step = pl.program_id(0)
    tops = [sum(sizes[:n]) for n in range(count)]

    @pl.when(step == 0)
    def _():
        for top, size, ref in zip(tops, sizes, ins):
            packed[top : top + size, :] = ref[...]
        total[...] = jnp.zeros_like(total)

    for p in range(pieces):

        @pl.when(step // per == p)
        def _():
            inner = jnp.maximum(dot(packed[...], first[p][...]), 0.0).astype(jnp.bfloat16)
            total[...] += dot(inner, second[p][...])

    @pl.when(step == pieces * per - 1)
    def _():
        for n, (top, size, ref) in enumerate(zip(tops, sizes, outs)):
            rows = size // max(1, len(slots[n]))
            for m, slot in enumerate(slots[n]):
                part = slice(top + m * rows, top + (m + 1) * rows)
                kept = jnp.where(live[slot] > 0, total[part, :], 0.0)
                ref[m * rows : (m + 1) * rows, :] = kept.astype(jnp.bfloat16)
            if not slots[n]:
                ref[...] = total[top : top + size, :].astype(jnp.bfloat16)


def expert_ffn(ins, first, second, live=None, slots=None):
    pieces, (width, hidden) = len(first), first[0].shape
    sizes = [a.shape[0] for a in ins]
    rows = sum(sizes)
    chunk = 1024 if rows <= 256 else 512
    chunk = chunk if hidden % chunk == 0 else hidden
    per = hidden // chunk
    if live is None:
        live, slots = jnp.zeros((1,), jnp.int32), [[]] * len(ins)

    def at(p, i):
        return jnp.clip(i - p * per, 0, per - 1)

    return pl.pallas_call(
        functools.partial(expert_kernel, sizes, pieces, per, slots),
        grid=(pieces * per,),
        in_specs=[pl.BlockSpec(memory_space=pltpu.SMEM)]
        + in_vmem(len(ins))
        + [pl.BlockSpec((width, chunk), lambda i, p=p: (0, at(p, i))) for p in range(pieces)]
        + [pl.BlockSpec((chunk, width), lambda i, p=p: (at(p, i), 0)) for p in range(pieces)],
        out_specs=in_vmem(len(ins)),
        out_shape=[jax.ShapeDtypeStruct(a.shape, jnp.bfloat16) for a in ins],
        scratch_shapes=[
            pltpu.VMEM((rows, width), jnp.bfloat16),
            pltpu.VMEM((rows, width), jnp.float32),
        ],
        compiler_params=pltpu.CompilerParams(
            dimension_semantics=("arbitrary",), vmem_limit_bytes=VMEM_LIMIT
        ),
        cost_estimate=cost(2 * rows * width * hidden * pieces, *first, *second),
    )(live, *ins, *map(hbm, first), *map(hbm, second))


def body(
    tokens,
    lengths,
    target,
    lang_group,
    blocks,
    enc_gain,
    w_query,
    w_key,
    w_value,
    w_output,
    moe_gain,
    expert_in,
    expert_out,
):
    count, width = tokens.shape
    lang_count, fsdp_count = lax.axis_size("lang"), lax.axis_size("fsdp")
    lang_at, fsdp_at = lax.axis_index("lang"), lax.axis_index("fsdp")
    slots_dev = min(32, lang_count // 2)
    capacity = count // slots_dev
    direct = lang_count <= 16 and lang_count & (lang_count - 1) == 0 and capacity % 16 == 0
    fsdp_scalar = fsdp_at.astype(jnp.int32).reshape(1)
    lang_scalar = lang_at.astype(jnp.int32).reshape(1)

    def others(shard):
        return [
            lax.ppermute(shard, "fsdp", [(i, (i + s) % fsdp_count) for i in range(fsdp_count)])
            for s in range(1, fsdp_count)
        ]

    ends = jnp.cumsum(lengths)
    positions = jnp.arange(count, dtype=jnp.int32)
    sentence = jnp.sum((positions[:, None] >= ends[None, :]).astype(jnp.int32), axis=1)
    lang_ids = jnp.arange(lang_group.shape[0], dtype=jnp.int32)
    sent_group = jnp.sum(
        jnp.where(target[:, None] == lang_ids[None, :], lang_group[None, :], 0), axis=1
    )
    run_ids = jnp.arange(slots_dev, dtype=jnp.int32)
    run_sent = jnp.sum((run_ids[:, None] * capacity >= ends[None, :]).astype(jnp.int32), axis=1)
    sent_ids = jnp.arange(lengths.shape[0], dtype=jnp.int32)
    run_group = jnp.sum(
        jnp.where(run_sent[:, None] == sent_ids[None, :], sent_group[None, :], 0), axis=1
    )
    group_ids = jnp.arange(lang_count, dtype=jnp.int32)
    half = lang_count // 2
    slot_group = jnp.where(
        group_ids < half,
        lang_at // half * half + group_ids,
        jnp.bitwise_xor(group_ids, lang_at.astype(jnp.int32)),
    )
    run_of_slot = slots_dev - jnp.sum(
        jnp.where(run_group[None, :] == slot_group[:, None], slots_dev - run_ids[None, :], 0),
        axis=1,
    )
    weights = (w_query, w_key, w_value)
    later = [others(w) for w in weights]
    output_w = [w_output, *others(w_output)]
    rest, sums = project(fsdp_scalar, tokens, enc_gain[None, :], weights, fsdp_count)
    block = 128 if count % 128 == 0 and 128 % capacity == 0 else count
    keys = sentence.reshape(count // block, 1, block)
    same = sentence.reshape(count // block, block, 1) == keys
    bias = jnp.where(same, jnp.float32(0), jnp.float32(-1e30)).reshape(count, block)
    bias, run_of_slot, later = lax.optimization_barrier((bias, run_of_slot, later))
    context = attend(bias, rest, sums, later)
    context, output_w, *shards = lax.optimization_barrier(
        (context, output_w, expert_in[0], expert_out[0])
    )
    first, second = ([shard, *others(shard)] for shard in shards)
    hidden, slots = hidden_states(
        fsdp_scalar, run_of_slot, context, tokens, moe_gain[None, :], output_w, slots_dev,
        lang_count if direct else 0,
    )

    def swap(ks, arrays):
        return [
            lax.ppermute(a, "lang", [(i, i ^ k) for i in range(lang_count)])
            for k, a in zip(ks, arrays)
        ]

    if direct:

        def within(array):
            halves = [list(range(top, top + half)) for top in (0, half)]
            return lax.all_to_all(
                array, "lang", 0, 0, axis_index_groups=halves, tiled=True
            )

        def after(arrays, *done):
            return list(lax.optimization_barrier((tuple(arrays), done))[0])

        quarter = half // 2
        far, last = range(half, half + quarter), range(half + quarter, lang_count)
        far_in = swap(far, slots[1 : 1 + quarter])
        near_in = within(slots[0])
        last_in = []
        for n, k in enumerate(last):
            done = far_in[min(n, quarter - 2)]
            last_in += swap([k], after([slots[1 + quarter + n]], done))
        far_out = expert_ffn(stage(far_in), first, second)
        far_out, live = live_rows(lang_scalar, blocks, near_in, [*far_in, *last_in], far_out)
        ins = after([near_in.reshape(half * capacity, width), *last_in], far_out)
        far_back = swap(far, far_out)
        held = [list(range(half)), *[[k] for k in last]]
        near_out, *last_out = after(expert_ffn(ins, first, second, live, held), far_back)
        last_back = swap(last, last_out)
        near_back = within(near_out.reshape(half, capacity, width))
        mixed = mix(run_of_slot[half + quarter :], hidden, last_back, slots_dev, AHEAD)
        return mix(run_of_slot, mixed, [near_back, *far_back], slots_dev)

    dispatch = (group_ids[:, None] == run_group[None, :]).astype(jnp.bfloat16)
    runs = slots[0].reshape(slots_dev, capacity * width)
    outgoing = jnp.dot(dispatch, runs, preferred_element_type=jnp.float32).astype(jnp.bfloat16)
    used = jnp.any(dispatch > 0, axis=1, keepdims=True)
    outgoing = jnp.where(used, outgoing, jnp.bfloat16(EMPTY))
    incoming = lax.all_to_all(
        outgoing.reshape(lang_count, capacity, width), "lang", 0, 0, tiled=True
    )
    full = (incoming[:, 0, 0] < EMPTY / 2).astype(jnp.int32)
    live = (jnp.cumsum(full) - full) * capacity // BLOCK < blocks[0, 0]
    (result,) = expert_ffn([incoming.reshape(lang_count * capacity, width)], first, second)
    result = jnp.where(live[:, None, None], result.reshape(lang_count, capacity, width), 0)
    back = lax.all_to_all(result.astype(jnp.bfloat16), "lang", 0, 0, tiled=True)
    expert = lax.dot_general(
        dispatch,
        back.reshape(lang_count, capacity * width),
        (((0,), (0,)), ((), ())),
        preferred_element_type=jnp.float32,
    ).reshape(count, width)
    return (hidden.astype(jnp.float32) + expert).astype(jnp.bfloat16)


def solution(mesh):
    return jax.shard_map(
        body,
        mesh=mesh,
        in_specs=(
            P(("lang", "fsdp"), None),
            P(("lang", "fsdp")),
            P(("lang", "fsdp")),
            P(),
            P("lang", "fsdp"),
            P(),
            P("fsdp", None),
            P("fsdp", None),
            P("fsdp", None),
            P("fsdp", None),
            P(),
            P("lang", None, "fsdp"),
            P("lang", "fsdp", None),
        ),
        out_specs=P(("lang", "fsdp"), None),
        check_vma=False,
    )
```
